128 devices in a mesh: ctx: 8 (over y, core), exp: 16 (over x, z).
Axes of the slice: x: 4, y: 4, z: 4, core: 2. Of those that a mesh axis runs over, the one named last changes fastest.
Arguments:
- query_rows: bfloat16 [4096, 8192], P('ctx', 'exp'), may hold values from -2 to 2
- key_rows: bfloat16 [4096, 8192], P('ctx', 'exp'), may hold values from -2 to 2
- value_rows: bfloat16 [4096, 8192], P('ctx', 'exp'), may hold values from -6 to 6
- log_decay: float32 [4096, 64], P('ctx', 'exp'), may hold values from -1 to 0, as said below
- attn_gain: float32 [8192], P('exp'), may hold values from 0.1 to 1.9
- out_weight: bfloat16 [8192, 6144], P('exp', 'ctx'), may hold values from -0.0625 to 0.0625
- residual: bfloat16 [4096, 6144], P(('ctx', 'exp')), may hold values from -6 to 6
- ffn_gain: float32 [6144], replicated, may hold values from 0.1 to 1.9
- router: float32 [6144, 16], replicated, may hold values from -0.21875 to 0.21875
- expert_ids: int32 [4096, 2], P('ctx'), may hold values from 0 to 15, all different within a row; in each aligned block of 512 rows (0 to 511, 512 to 1023, ...) at most 80 rows name the same one
- w_gate: bfloat16 [16, 6144, 4608], P('exp', None, 'ctx'), may hold values from -0.078125 to 0.078125
- w_up: bfloat16 [16, 6144, 4608], P('exp', None, 'ctx'), may hold values from -0.078125 to 0.078125
- w_down: bfloat16 [16, 4608, 6144], P('exp', 'ctx'), may hold values from -0.09375 to 0.09375
Outputs:
- mixed: bfloat16 [4096, 6144], P(('ctx', 'exp'))
The draws below stay inside these ranges and needn't reach their ends.
Inputs may be any that keep to these rules, and one draw needn't show every extreme that they name: `expert_ids`: each row names two different experts. Within the 512 rows of each block no expert is named by more than 80 rows, and in some block one expert is named by exactly 80. `log_decay`: strictly negative.
All inputs are finite; a program needn't handle non-finite values.
Results may differ from the reference program's by a relative error of at most 0.024.
Values may be sent and summed in bfloat16 or wider, within the bound.
A program may use at most 128 MiB of HBM per device.

```python
import math
import jax
import jax.numpy as jnp
import numpy as np
from jax import lax

D = 6144
HEADS = 64
HEAD_DIM = 128
FF = 4608
TOK_CTX = 512
EXPERTS = 16
CAP = 80
TOKENS = 4096
N_CTX = 8


def draw_log_decay(key, part):
    key = jax.random.fold_in(key, 11)
    keys = jax.random.split(key, 6)
    fast_share = 0.5
    fast = jax.random.bernoulli(keys[0], fast_share, (HEADS,))
    slow_rate = jax.random.uniform(keys[1], (HEADS,), minval=0.2, maxval=0.6) / TOKENS
    fast_rate = jnp.exp(jax.random.uniform(keys[2], (HEADS,), minval=math.log(1.0 / 50.0), maxval=math.log(1.0 / 30.0)))
    starting_shift = jnp.where(fast, fast_rate, slow_rate)
    approximate_guess = jnp.exp(jax.random.uniform(keys[3], (TOKENS, HEADS), minval=-0.7, maxval=0.7))
    capacity_places = jax.random.randint(keys[4], (2, HEADS), 0, TOKENS)
    sequence_place = lax.broadcasted_iota(jnp.int32, (TOKENS, HEADS), 0)
    segment_span = (sequence_place == capacity_places[0][None, :]) | (sequence_place == capacity_places[1][None, :])
    objective_number = jnp.log(jax.random.uniform(keys[5], (TOKENS, HEADS), minval=0.55, maxval=0.8))
    return (-starting_shift[None, :] * approximate_guess + jnp.where(segment_span, objective_number, 0.0)).astype(jnp.float32)


def level_of(own_key, shape, cuts, least, high):
    def one(position, shards_of):
        steps = jax.random.uniform(jax.random.fold_in(jax.random.fold_in(own_key, 6), position), (shards_of,), jnp.float32, least / len(cuts), high / len(cuts))
        return jnp.repeat(jnp.exp(steps), shape[position] // shards_of).reshape((-1,) + (1,) * (len(shape) - position - 1))

    loudness = one(*cuts[0])
    for cut in cuts[1:]:
        loudness = loudness * one(*cut)
    return loudness


def assign_block(stream_key, own, number, rows, count, top, reach, slope):
    ranking = jax.random.permutation(stream_key, count)
    packed, usual = portions_of(count, rows * top, reach, slope, True), portions_of(count, rows * top, reach, slope, False)
    places = jnp.arange(count)

    def named(lengths, rotation):
        used = int((lengths > 0).sum())
        fixed = max(1, used // 4)
        passed = fixed + (places - fixed + rotation * (used - fixed)) % max(1, count - fixed)
        return jnp.zeros((count,), jnp.int32).at[ranking[jnp.where(places < fixed, places, passed)]].set(jnp.asarray(lengths, jnp.int32))

    lengths = jnp.where(number % 4 == 0, named(packed, number // 4), named(usual, number - number // 4 - 1))
    mixed = jax.random.permutation(jax.random.fold_in(own, 3), count)
    donor, receiver = mixed[0:count // 2 * 2:2], mixed[1:count // 2 * 2:2]
    room = jnp.minimum(lengths[donor] - 1, reach - lengths[receiver]) // 2
    room = jnp.where((donor == ranking[0]) | (receiver == ranking[0]) | (lengths[receiver] == 0), 0, jnp.maximum(room, 0))
    passed = jax.random.randint(jax.random.fold_in(own, 4), (count // 2,), 0, 1 << 20) % (room + 1)
    lengths = lengths.at[donor].add(-passed).at[receiver].add(passed)
    items = jnp.searchsorted(jnp.cumsum(lengths), jnp.arange(rows * top), side="right").astype(jnp.int32)
    table = items.reshape(top, rows).T
    table = table[jax.random.permutation(jax.random.fold_in(own, 1), rows)]
    rotation = jax.random.randint(jax.random.fold_in(own, 2), (rows, 1), 0, top)
    return jnp.take_along_axis(table, (jnp.arange(top)[None, :] + rotation) % top, axis=1)


def portions_of(number_of, total, bound, lean, full):
    loads = [(1 << 20) // math.isqrt(grade ** lean) + 1 for grade in range(1, number_of + 1)]
    largest = bound if full else min(bound, max(-(-total // number_of), total * loads[0] // sum(loads)))
    least = 1 if total - largest >= number_of - 1 else 0
    holding, spare = [largest] + [least] * (number_of - 1), total - largest - least * (number_of - 1)
    while spare > 0:
        movable = [i for i in range(1, number_of) if holding[i] < largest] or [i for i in range(1, number_of) if holding[i] < bound]
        pool, left = sum([loads[i] for i in movable]), spare
        for i in movable:
            more = min(bound - holding[i], max(1, left * loads[i] // pool), spare)
            holding[i] = holding[i] + more
            spare = spare - more
    return np.array(holding)


def centred(stream_key, shape, scale, reach, shards=(), kind=jnp.bfloat16):
    level = level_of(stream_key, shape, shards, -0.22, 0.18) if shards else 1.0
    values = jax.random.normal(stream_key, shape, jnp.float32) * scale * level
    return jnp.minimum(jnp.maximum(values, -reach), reach).astype(kind)


def setup_inputs(seed: int = 0) -> dict:
    key_of = jax.random.split(jax.random.key(seed), 14)
    query_rows = centred(key_of[0], (TOKENS, HEADS * HEAD_DIM), 0.3, 2.0, ((0, 8), (1, 16)))
    key_rows = centred(key_of[1], (TOKENS, HEADS * HEAD_DIM), 0.3, 2.0, ((0, 8), (1, 16)))
    value_rows = centred(key_of[2], (TOKENS, HEADS * HEAD_DIM), 1.0, 6.0, ((0, 8), (1, 16)))
    log_decay = draw_log_decay(jax.random.fold_in(key_of[13], 71), 0)
    attn_gain = jnp.clip(1.0 + 0.18 * jax.random.normal(key_of[4], (HEADS * HEAD_DIM,), jnp.float32), 0.1, 1.9)
    out_weight = centred(key_of[5], (HEADS * HEAD_DIM, D), (HEADS * HEAD_DIM) ** -0.5, 0.0625, ((0, 16), (1, 8)))
    residual = centred(key_of[6], (TOKENS, D), 1.0, 6.0, ((0, 128),))
    ffn_gain = jnp.clip(1.0 + 0.18 * jax.random.normal(key_of[7], (D,), jnp.float32), 0.1, 1.9)
    router = centred(key_of[8], (D, EXPERTS), (D // 9) ** -0.5, 0.21875, (), jnp.float32)
    expert_ids_keys = jax.random.split(jax.random.fold_in(key_of[9], 1), TOKENS // TOK_CTX)
    expert_ids_turns = jax.random.permutation(jax.random.fold_in(key_of[9], 3), TOKENS // TOK_CTX)
    expert_ids = jax.vmap(lambda own, number: assign_block(jax.random.fold_in(key_of[9], 2), own, number, TOK_CTX, EXPERTS, 2, CAP, 2))(expert_ids_keys, expert_ids_turns).reshape((TOKENS, 2))
    w_gate = centred(key_of[10], (EXPERTS, D, FF), D ** -0.5, 0.078125, ((0, 16), (2, 8)))
    w_up = centred(key_of[11], (EXPERTS, D, FF), D ** -0.5, 0.078125, ((0, 16), (2, 8)))
    w_down = centred(key_of[12], (EXPERTS, FF, D), FF ** -0.5, 0.09375, ((0, 16), (1, 8)))
    return {"query_rows": query_rows, "key_rows": key_rows, "value_rows": value_rows, "log_decay": log_decay, "attn_gain": attn_gain, "out_weight": out_weight, "residual": residual, "ffn_gain": ffn_gain, "router": router, "expert_ids": expert_ids, "w_gate": w_gate, "w_up": w_up, "w_down": w_down}


def block_terms(queries, keys_all, values_all, log_decay):
    length = queries.shape[0]
    running = jnp.cumsum(log_decay, axis=0)
    later_pos = lax.broadcasted_iota(jnp.int32, (length, length), 0)
    earlier_pos = lax.broadcasted_iota(jnp.int32, (length, length), 1)
    spread = jnp.transpose(running)[:, :, None] - jnp.transpose(running)[:, None, :]
    decay = jnp.where((later_pos >= earlier_pos)[None], jnp.exp(jnp.minimum(spread, 0.0)), 0.0)
    scores = jnp.einsum('thd,shd->hts', queries.astype(jnp.float32), keys_all.astype(jnp.float32), precision=lax.Precision.HIGHEST)
    weights = (scores * decay).astype(jnp.bfloat16)
    inner = jnp.einsum('hts,shd->thd', weights.astype(jnp.float32), values_all.astype(jnp.float32), precision=lax.Precision.HIGHEST)
    to_end = jnp.exp(running[-1][None, :] - running)
    decayed_keys = (keys_all.astype(jnp.float32) * to_end[:, :, None]).astype(jnp.bfloat16)
    own_state = jnp.einsum('shd,she->hde', decayed_keys.astype(jnp.float32), values_all.astype(jnp.float32), precision=lax.Precision.HIGHEST)
    return (running, inner, own_state)

def head_norm(values, gain):
    squares = lax.optimization_barrier(jnp.mean(values * values, axis=-1, keepdims=True))
    scaled = values * lax.rsqrt(squares + 1e-06) * gain.reshape(1, values.shape[1], -1)
    return scaled.astype(jnp.bfloat16).reshape(values.shape[0], -1)

def row_norm(rows, gain):
    values = rows.astype(jnp.float32)
    squares = lax.optimization_barrier(jnp.mean(values * values, axis=-1, keepdims=True))
    return (values * lax.rsqrt(squares + 1e-05) * gain).astype(jnp.bfloat16)

def reference(query_rows, key_rows, value_rows, log_decay, attn_gain, out_weight, residual, ffn_gain, router, expert_ids, w_gate, w_up, w_down):
    shape4 = (N_CTX, TOK_CTX, HEADS, HEAD_DIM)
    query_blocks = query_rows.reshape(shape4)
    key_blocks = key_rows.reshape(shape4)
    value_blocks = value_rows.reshape(shape4)
    decay_blocks = log_decay.reshape(N_CTX, TOK_CTX, HEADS)

    def attend(carried, inputs):
        queries, keys_all, values_all, decays = inputs
        running, inner, own_state = block_terms(queries, keys_all, values_all, decays)
        scaled_query = queries.astype(jnp.float32) * jnp.exp(running)[:, :, None]
        cross = jnp.einsum('thd,hde->the', scaled_query, carried, precision=lax.Precision.HIGHEST)
        attn_rows = head_norm(inner + cross, attn_gain)
        following = jnp.exp(running[-1])[:, None, None] * carried + own_state
        return (following, attn_rows)
    start_state = jnp.zeros((HEADS, HEAD_DIM, HEAD_DIM), jnp.float32)
    _, attn_out = lax.scan(attend, start_state, (query_blocks, key_blocks, value_blocks, decay_blocks))
    attn_out = attn_out.reshape(TOKENS, HEADS * HEAD_DIM)
    mapped_vectors = jnp.dot(attn_out, out_weight, preferred_element_type=jnp.float32)
    hidden = (residual.astype(jnp.float32) + mapped_vectors).astype(jnp.bfloat16)
    normed = row_norm(hidden, ffn_gain)
    logits = jnp.dot(normed.astype(jnp.float32), router, precision=lax.Precision.HIGHEST)
    table = expert_ids[:, :, None] == jnp.arange(EXPERTS, dtype=jnp.int32)[None, None, :]
    chosen = lax.optimization_barrier(jnp.sum(jnp.where(table, logits[:, None, :], 0.0), axis=-1))
    gates = jax.nn.sigmoid(chosen)
    shares = gates / lax.optimization_barrier(jnp.sum(gates, axis=1, keepdims=True))
    id_blocks = expert_ids.reshape(N_CTX, TOK_CTX, 2)
    share_blocks = shares.reshape(N_CTX, TOK_CTX, 2)
    normed_blocks = normed.reshape(N_CTX, TOK_CTX, D).astype(jnp.float32)
    width = FF // N_CTX

    def single_specialist(total, expert):
        match = id_blocks == expert
        picked = jnp.any(match, axis=-1).astype(jnp.int32)
        rank = jnp.cumsum(picked, axis=1, dtype=jnp.int32) - picked
        slots = jnp.arange(CAP, dtype=jnp.int32)
        onehot = ((rank[:, None, :] == slots[None, :, None]) & (picked[:, None, :] > 0)).astype(jnp.float32)
        dispatched = jnp.einsum('bjt,btd->bjd', onehot, normed_blocks, precision=lax.Precision.HIGHEST).astype(jnp.bfloat16).reshape(N_CTX * CAP, D)
        gate_all = w_gate[expert]
        up_all = w_up[expert]
        down_all = w_down[expert]
        summed = jnp.zeros((N_CTX * CAP, D), jnp.float32)
        for index in range(N_CTX):
            gate = jnp.dot(dispatched, gate_all[:, index * width:(index + 1) * width], preferred_element_type=jnp.float32)
            upper = jnp.dot(dispatched, up_all[:, index * width:(index + 1) * width], preferred_element_type=jnp.float32)
            activated = (jax.nn.silu(gate) * upper).astype(jnp.bfloat16)
            piece = jnp.dot(activated, down_all[index * width:(index + 1) * width, :], preferred_element_type=jnp.float32)
            summed = summed + lax.optimization_barrier(piece.astype(jnp.bfloat16)).astype(jnp.float32)
        expert_out = summed.astype(jnp.bfloat16).reshape(N_CTX, CAP, D).astype(jnp.float32)
        mine = lax.optimization_barrier(jnp.sum(jnp.where(match, share_blocks, 0.0), axis=-1))
        returned_output = jnp.einsum('bjt,bjd->btd', onehot, expert_out, precision=lax.Precision.HIGHEST) * mine[:, :, None]
        total = total + lax.optimization_barrier(returned_output.astype(jnp.bfloat16)).astype(jnp.float32)
        return (total, None)
    total, _ = lax.scan(single_specialist, jnp.zeros((N_CTX, TOK_CTX, D), jnp.float32), jnp.arange(EXPERTS, dtype=jnp.int32))
    return (hidden.astype(jnp.float32) + total.reshape(TOKENS, D)).astype(jnp.bfloat16)
```

```python
import functools

import jax
import jax.numpy as jnp
from jax import lax
from jax.experimental import pallas as pl
from jax.experimental.pallas import tpu as pltpu
from jax.sharding import PartitionSpec as P

MESH = pl.DeviceIdType.MESH
F32 = jnp.float32
BF16 = jnp.bfloat16
EXPERTS = 16
CAP = 80
UNIT = 384
LINKS = 128


def place():
    ctx = lax.axis_index("ctx")
    exp = lax.axis_index("exp")
    return ctx // 2, ctx % 2, exp // 4, exp % 4


def along(axis, step):
    y, core, x, z = place()
    step = step % 4
    if axis == "x":
        return (y * 2 + core, (x + step) % 4 * 4 + z)
    if axis == "z":
        return (y * 2 + core, x * 4 + (z + step) % 4)
    return ((y + step) % 4 * 2 + core, x * 4 + z)


def exp_peer(step):
    return (lax.axis_index("ctx"), (lax.axis_index("exp") + step) % EXPERTS)


def other_core():
    y, core, _, _ = place()
    return (y * 2 + 1 - core, lax.axis_index("exp"))


class Links:
    def __init__(self, send, recv):
        self.send, self.recv, self.count, self.open = send, recv, 0, []

    def copy(self, src, dst, device):
        made = pltpu.make_async_remote_copy(
            src_ref=src,
            dst_ref=dst,
            send_sem=self.send.at[self.count],
            recv_sem=self.recv.at[self.count],
            device_id=device,
            device_id_type=MESH,
        )
        made.start()
        self.count += 1
        self.open.append(made)
        return made

    def drain(self):
        for made in self.open:
            made.wait_send()
        self.open = []


def add_into(target, extra):
    size = 128 if target.shape[0] % 128 == 0 else 80

    def one(i, carry):
        rows = rows_at(i * size, size)
        target[rows, :] = (target[rows, :].astype(F32) + extra[rows, :].astype(F32)).astype(BF16)
        return carry

    lax.fori_loop(0, target.shape[0] // size, one, 0)


class RingSum:
    def __init__(self, links, axis, part, base, n, first, second):
        place_of = dict(zip(("y", "core", "x", "z"), place()))
        self.links, self.axis, self.i = links, axis, place_of[axis]
        self.part, self.base, self.n = part, base, n
        self.first, self.second = first, second

    def low(self, d):
        return self.part.at[rows_at(self.base + d * self.n, self.n // 2)]

    def high(self, d):
        return self.part.at[rows_at(self.base + d * self.n + self.n // 2, self.n // 2)]

    def slot(self, k):
        return pl.ds(k * (self.n // 2), self.n // 2)

    def opposite(self):
        far, slot = (self.i + 2) % 4, self.slot
        up = self.links.copy(self.low(far), self.first.at[slot(0)], along(self.axis, 1))
        down = self.links.copy(self.high(far), self.first.at[slot(1)], along(self.axis, -1))
        self.far = (up, down)

    def direct(self):
        up, down, slot = (self.i + 1) % 4, (self.i + 3) % 4, self.slot
        self.near = [
            self.links.copy(self.high(up), self.second.at[slot(1)], along(self.axis, 1)),
            self.links.copy(self.low(down), self.second.at[slot(2)], along(self.axis, -1)),
        ]

    def relay(self):
        up, down, slot = (self.i + 1) % 4, (self.i + 3) % 4, self.slot
        self.far[0].wait_recv()
        add_into(self.low(up), self.first.at[slot(0)])
        self.near.append(
            self.links.copy(self.low(up), self.second.at[slot(0)], along(self.axis, 1))
        )
        self.far[1].wait_recv()
        add_into(self.high(down), self.first.at[slot(1)])
        self.near.append(
            self.links.copy(self.high(down), self.second.at[slot(3)], along(self.axis, -1))
        )

    def arrived(self):
        for made in self.near:
            made.wait_recv()

    def total(self, start, size):
        own = self.part[rows_at(self.base + self.i * self.n + start, size), :].astype(F32)
        own = own + self.second[rows_at(start, size), :].astype(F32)
        return own + self.second[rows_at(self.n + start, size), :].astype(F32)


def columns(start, size):
    return pl.ds(pl.multiple_of(start, 128), size)


def rows_at(start, size):
    return pl.ds(pl.multiple_of(start, 16), size)


def layer_kernel(
    attn_ref,
    out_w_ref,
    resid_ref,
    ids_ref,
    gain_ref,
    router_ref,
    gate_ref,
    up_ref,
    down_ref,
    out_ref,
    wide,
    gate_up,
    work,
    first_a,
    first_b,
    second_a,
    second_b,
    half_a,
    half_b,
    last_first_a,
    last_first_b,
    last_second_a,
    last_second_b,
    resid_cols,
    hidden,
    table,
    pieces,
    rows_in,
    tokens,
    active,
    partner,
    first_y,
    second_y,
    back,
    mixed,
    rows_out,
    local,
    send,
    recv,
):
    y, core, x, z = place()
    ctx = y * 2 + core
    me = lax.axis_index("exp")
    links = Links(send, recv)

    load_w = pltpu.make_async_copy(out_w_ref, wide.at[:, pl.ds(0, 512)], local.at[0])
    load_w.start()
    load_gate = pltpu.make_async_copy(gate_ref, gate_up.at[pl.ds(0, 576)], local.at[1])
    load_up = pltpu.make_async_copy(up_ref, gate_up.at[pl.ds(576, 576)], local.at[2])

    barrier = pltpu.get_barrier_semaphore()
    for step in range(1, EXPERTS):
        pl.semaphore_signal(barrier, inc=1, device_id=exp_peer(step), device_id_type=MESH)
    for device in (along("y", 1), along("y", -1), other_core()):
        pl.semaphore_signal(barrier, inc=1, device_id=device, device_id_type=MESH)
    pl.semaphore_wait(barrier, EXPERTS + 2)

    resid_moves = []
    for step in range(1, EXPERTS):
        to = (me + step) % EXPERTS
        resid_moves.append(
            links.copy(
                resid_ref.at[:, columns(to * UNIT, UNIT)],
                resid_cols.at[rows_at(me * 32, 32)],
                exp_peer(step),
            )
        )
    resid_cols[rows_at(me * 32, 32), :] = resid_ref[:, columns(me * UNIT, UNIT)]

    load_w.wait()
    load_gate.start()
    load_up.start()

    def keep(base, r, u):
        for half in range(2):
            for side in range(2):
                to = base + (side * 4 + u + half) * 128
                work[rows_at(to, 128), :] = r[
                    side * 128 : side * 128 + 128, half * UNIT : half * UNIT + UNIT
                ].astype(BF16)

    def project_a(to):
        def one(h, carry):
            w = wide[to * 2 + h, pl.ds(0, 512), :]
            r = jnp.dot(attn_ref[pl.ds(0, 256), :], w, preferred_element_type=F32)
            keep(to * 1024, r, h * 2)
            return carry

        lax.fori_loop(0, 2, one, 0)

    def project_b(pair):
        def one(to, carry):
            w = wide[to * 2 + pair, pl.ds(0, 512), :]
            r = jnp.dot(attn_ref[pl.ds(256, 256), :], w, preferred_element_type=F32)
            for half in range(2):
                for side in range(2):
                    start = 4096 + (pair * 2 + half) * 1024 + (side * 4 + to) * 128
                    work[rows_at(start, 128), :] = r[
                        side * 128 : side * 128 + 128, half * UNIT : half * UNIT + UNIT
                    ].astype(BF16)
            return carry

        lax.fori_loop(0, 4, one, 0)

    ring_a = RingSum(links, "x", work, 0, 1024, first_a, second_a)
    ring_b = RingSum(links, "z", work, 4096, 1024, first_b, second_b)
    project_a((x + 2) % 4)
    ring_a.opposite()
    far_pair = (z + 2) % 4 // 2
    project_b(far_pair)
    ring_b.opposite()
    project_a((x + 1) % 4)
    project_a((x + 3) % 4)
    ring_a.direct()
    project_b(1 - far_pair)
    ring_b.direct()
    project_a(x)
    load_down = []
    for s in range(8):
        made = pltpu.make_async_copy(
            down_ref.at[:, pl.ds(s * 768, 768)], wide.at[s], local.at[3 + s]
        )
        made.start()
        load_down.append(made)

    experts = lax.broadcasted_iota(jnp.int32, (EXPERTS, 512), 0)
    picked = (ids_ref[0:1, :] == experts) | (ids_ref[1:2, :] == experts)
    before = lax.broadcasted_iota(jnp.int32, (512, 512), 0) < lax.broadcasted_iota(
        jnp.int32, (512, 512), 1
    )
    rank = jnp.dot(
        jnp.where(picked, 1.0, 0.0).astype(BF16),
        jnp.where(before, 1.0, 0.0).astype(BF16),
        preferred_element_type=F32,
    )
    code = jnp.where(picked, rank, -1.0)
    slots = lax.broadcasted_iota(jnp.int32, (CAP, 512), 0).astype(F32)
    for e in range(EXPERTS):
        table[pl.ds(e * CAP, CAP), :] = jnp.where(code[e : e + 1, :] == slots, 1.0, 0.0).astype(
            BF16
        )

    ring_a.relay()
    ring_b.relay()

    def gather_sum(ring, target):
        ring.arrived()

        def one(u, carry):
            for side in range(2):
                rows = rows_at(u * 256 + side * 128, 128)
                target[rows, :] = ring.total(side * 512 + u * 128, 128).astype(BF16)
            return carry

        lax.fori_loop(0, 4, one, 0)

    last_a = RingSum(links, "z", half_a, 0, 256, last_first_a, last_second_a)
    last_b = RingSum(links, "x", half_b, 0, 256, last_first_b, last_second_b)
    gather_sum(ring_a, half_a)
    last_a.opposite()
    last_a.direct()
    gather_sum(ring_b, half_b)
    last_b.opposite()
    last_b.direct()
    last_a.relay()
    last_b.relay()
    for made in resid_moves:
        made.wait_recv()

    def finish_sum(ring, start):
        ring.arrived()
        rows = pl.ds(start, 256)
        hidden[rows, :] = (ring.total(0, 256) + resid_cols[rows, :].astype(F32)).astype(BF16)

    finish_sum(last_a, 0)
    finish_sum(last_b, 256)

    def rows_for(e):
        t = table[rows_at(e * CAP, CAP), :]
        return jnp.dot(t, hidden[...], preferred_element_type=F32).astype(BF16)

    row_moves = []
    for step in range(1, EXPERTS):
        piece = pl.ds(step * CAP, CAP)
        pieces[piece, :] = rows_for((me + step) % EXPERTS)
        row_moves.append(
            links.copy(
                pieces.at[piece], rows_in.at[:, columns(me * UNIT, UNIT)], exp_peer(step)
            )
        )
    rows_in[:, columns(me * UNIT, UNIT)] = rows_for(me)
    my_table = table[rows_at(me * CAP, CAP), :]
    my_ids = lax.dot_general(
        my_table,
        ids_ref[...].astype(F32).astype(BF16),
        (((1,), (1,)), ((), ())),
        preferred_element_type=F32,
    )
    router_high = router_ref[...].astype(BF16)
    router_low = (router_ref[...] - router_high.astype(F32)).astype(BF16)
    for made in row_moves:
        made.wait_recv()

    links.drain()

    mine = rows_at(ctx * CAP, CAP)
    squares = jnp.zeros((CAP, 1), F32)
    for u in range(EXPERTS):
        part = rows_in[:, pl.ds(u * UNIT, UNIT)].astype(F32)
        squares = squares + jnp.sum(part * part, axis=1, keepdims=True)
    scale = lax.rsqrt(squares / 6144.0 + 1e-05)
    for u in range(EXPERTS):
        cols = pl.ds(u * UNIT, UNIT)
        part = rows_in[:, cols].astype(F32)
        tokens[mine, cols] = (part * scale * gain_ref[:, cols]).astype(BF16)

    low, high = pl.ds(0, 3072), pl.ds(3072, 3072)

    def spread(block, cols, device):
        ref = tokens.at[rows_at(block * CAP, CAP), cols]
        return links.copy(ref, ref, device)

    above, below, far = (y + 1) % 4, (y + 3) % 4, (y + 2) % 4
    pair_own = spread(ctx, pl.ds(0, 6144), other_core())
    up_low = spread(ctx, low, along("y", 1))
    down_high = spread(ctx, high, along("y", -1))
    up_high = spread(ctx, high, along("y", 1))
    down_low = spread(ctx, low, along("y", -1))

    normed = tokens[mine, :]
    turned = (((1,), (1,)), ((), ()))
    logits = lax.dot_general(normed, router_high, turned, preferred_element_type=F32)
    logits = logits + lax.dot_general(normed, router_low, turned, preferred_element_type=F32)
    gates = 1.0 / (1.0 + jnp.exp(-logits))
    lanes = lax.broadcasted_iota(jnp.int32, (CAP, EXPERTS), 1)
    lanes_f = lanes.astype(F32)
    both = (my_ids[:, 0:1] == lanes_f) | (my_ids[:, 1:2] == lanes_f)
    total = jnp.sum(jnp.where(both, gates, 0.0), axis=1, keepdims=True)
    share = jnp.sum(jnp.where(lanes == me, gates, 0.0), axis=1, keepdims=True) / total

    load_gate.wait()
    load_up.wait()
    for made in load_down:
        made.wait()

    def gate_and_up(chip):
        rows = rows_at(chip * (2 * CAP), 2 * CAP)
        r = lax.dot_general(tokens[rows, :], gate_up[...], turned, preferred_element_type=F32)
        gate, upper = r[:, :576], r[:, 576:]
        active[...] = (gate / (1.0 + jnp.exp(-gate)) * upper).astype(BF16)

    block = EXPERTS * CAP

    def down(chip):
        def one(s, carry):
            o = jnp.dot(active[...], wide[s], preferred_element_type=F32).astype(BF16)
            for owner in range(2):
                for half in range(2):
                    start = (owner * 4 + chip) * block + (s * 2 + half) * CAP
                    work[rows_at(start, CAP), :] = o[
                        owner * CAP : owner * CAP + CAP, half * UNIT : half * UNIT + UNIT
                    ]
            return carry

        lax.fori_loop(0, 8, one, 0)
        return links.copy(
            work.at[rows_at(((1 - core) * 4 + chip) * block, block)],
            partner.at[rows_at(chip * block, block)],
            other_core(),
        )

    def join(chip, made):
        made.wait_recv()
        add_into(
            work.at[rows_at((core * 4 + chip) * block, block)],
            partner.at[rows_at(chip * block, block)],
        )

    pair_own.wait_recv()
    gate_and_up(y)
    sum_own = down(y)
    from_below, from_above, from_far = below * 2 + core, above * 2 + core, far * 2 + core
    up_low.wait_recv()
    on_up = spread(from_below, low, along("y", 1))
    pair = [spread(from_below, low, other_core())]
    down_high.wait_recv()
    on_down = spread(from_above, high, along("y", -1))
    pair.append(spread(from_above, high, other_core()))
    join(y, sum_own)
    up_high.wait_recv()
    pair.append(spread(from_below, high, other_core()))
    down_low.wait_recv()
    pair.append(spread(from_above, low, other_core()))
    for made in pair:
        made.wait_recv()
    gate_and_up(above)
    sum_above = down(above)
    gate_and_up(below)
    on_up.wait_recv()
    pair_far = [spread(from_far, low, other_core())]
    on_down.wait_recv()
    pair_far.append(spread(from_far, high, other_core()))
    sum_below = down(below)
    ring_y = RingSum(links, "y", work, core * (4 * block), block, first_y, second_y)
    join(above, sum_above)
    join(below, sum_below)
    ring_y.direct()
    for made in pair_far:
        made.wait_recv()
    gate_and_up(far)
    sum_far = down(far)
    join(far, sum_far)
    ring_y.opposite()
    ring_y.relay()
    ring_y.arrived()

    back_moves = []
    for step in range(EXPERTS):
        to = (me + step) % EXPERTS
        total = ring_y.total(to * CAP, CAP).astype(BF16).astype(F32)
        piece = pl.ds(step * CAP, CAP)
        if step == 0:
            back[rows_at(me * CAP, CAP), :] = (total * share).astype(BF16)
            continue
        pieces[piece, :] = (total * share).astype(BF16)
        back_moves.append(
            links.copy(pieces.at[piece], back.at[rows_at(me * CAP, CAP)], exp_peer(step))
        )
    for made in back_moves:
        made.wait_recv()
    first = (((0,), (0,)), ((), ()))
    summed = lax.dot_general(table[...], back[...], first, preferred_element_type=F32)
    mixed[...] = (hidden[...].astype(F32) + summed).astype(BF16)

    out_moves = []
    for step in range(1, EXPERTS):
        to = (me + step) % EXPERTS
        out_moves.append(
            links.copy(
                mixed.at[rows_at(to * 32, 32)],
                rows_out.at[:, columns(me * UNIT, UNIT)],
                exp_peer(step),
            )
        )
    rows_out[:, columns(me * UNIT, UNIT)] = mixed[rows_at(me * 32, 32), :]
    for made in out_moves:
        made.wait_recv()
    out_ref[...] = rows_out[...]
    links.drain()


def layer(attn_out, out_full, residual, ids, gain, router, gate, up, down):
    vmem = pl.BlockSpec(memory_space=pltpu.VMEM)
    hbm = pl.BlockSpec(memory_space=pl.ANY)

    def rows(n, width=UNIT):
        return pltpu.VMEM((n, width), BF16)

    block = EXPERTS * CAP
    return pl.pallas_call(
        layer_kernel,
        out_shape=jax.ShapeDtypeStruct((32, 6144), BF16),
        in_specs=[vmem, hbm, vmem, vmem, vmem, vmem, hbm, hbm, hbm],
        out_specs=vmem,
        scratch_shapes=[
            pltpu.VMEM((8, 576, 768), BF16),
            rows(1152, 6144),
            rows(8 * block),
            rows(1024),
            rows(1024),
            rows(2048),
            rows(2048),
            rows(1024),
            rows(1024),
            rows(256),
            rows(256),
            rows(512),
            rows(512),
            rows(512),
            rows(512),
            rows(block, 512),
            rows(block),
            rows(CAP, 6144),
            rows(8 * CAP, 6144),
            rows(2 * CAP, 576),
            rows(4 * block),
            rows(block),
            rows(2 * block),
            rows(block),
            rows(512),
            rows(32, 6144),
            pltpu.SemaphoreType.DMA((11,)),
            pltpu.SemaphoreType.DMA((LINKS,)),
            pltpu.SemaphoreType.DMA((LINKS,)),
        ],
        compiler_params=pltpu.CompilerParams(
            collective_id=0, has_side_effects=True, vmem_limit_bytes=62 << 20
        ),
        name="layer",
    )(attn_out, out_full, residual, ids, gain, router, gate, up, down)


def prefix(array, axis, join, neutral):
    place = lax.axis_index(axis)
    gathered = jax.tree.map(
        lambda a, kind: lax.all_gather(a.astype(kind), axis), array, (jnp.bfloat16, jnp.bfloat16)
    )
    state = jax.tree.map(lambda a, e: jnp.zeros_like(a) + jnp.asarray(e, a.dtype), array, neutral)

    def one(lap, state):
        return join(
            state,
            jax.tree.map(
                lambda a, own: lax.dynamic_index_in_dim(a, lap, 0, False).astype(own.dtype),
                gathered,
                array,
            ),
        )

    return lax.fori_loop(0, place, one, state)


def head_norm(values, gain):
    squares = jnp.mean(values * values, axis=-1, keepdims=True)
    scaled = values * lax.rsqrt(squares + 1e-06) * gain.reshape(1, values.shape[1], -1)
    return scaled.astype(jnp.bfloat16).reshape(values.shape[0], -1)


def chain_step(earlier, later):
    return (earlier[0] + later[0], jnp.exp(later[0])[:, None, None] * earlier[1] + later[1])


def per_device(
    query_rows,
    key_rows,
    value_rows,
    log_decay,
    attn_gain,
    out_weight,
    residual,
    ffn_gain,
    router,
    expert_ids,
    w_gate,
    w_up,
    w_down,
):
    length = query_rows.shape[0]
    heads = log_decay.shape[1]
    queries = query_rows.reshape(length, heads, -1)
    keys_all = key_rows.reshape(length, heads, -1)
    values_all = value_rows.reshape(length, heads, -1)
    running = jnp.cumsum(log_decay, axis=0)
    later_pos = lax.broadcasted_iota(jnp.int32, (length, length), 0)
    earlier_pos = lax.broadcasted_iota(jnp.int32, (length, length), 1)
    spread = jnp.transpose(running)[:, :, None] - jnp.transpose(running)[:, None, :]
    decay = jnp.where((later_pos >= earlier_pos)[None], jnp.exp(jnp.minimum(spread, 0.0)), 0.0)
    scores = jnp.einsum("thd,shd->hts", queries, keys_all, preferred_element_type=jnp.float32)
    weights = (scores * decay).astype(jnp.bfloat16)
    inner = jnp.einsum("hts,shd->thd", weights, values_all, preferred_element_type=jnp.float32)
    to_end = jnp.exp(running[-1][None, :] - running)
    decayed_keys = (keys_all.astype(jnp.float32) * to_end[:, :, None]).astype(jnp.bfloat16)
    own_state = jnp.einsum(
        "shd,she->hde", decayed_keys, values_all, preferred_element_type=jnp.float32
    )
    block_decay = running[-1]
    identity = (jnp.zeros_like(block_decay), jnp.zeros_like(own_state))
    carried = prefix((block_decay, own_state), "ctx", chain_step, identity)[1]
    scaled_query = queries.astype(jnp.float32) * jnp.exp(running)[:, :, None]
    cross = jnp.einsum("thd,hde->the", scaled_query, carried, precision=lax.Precision.HIGHEST)
    attn_out = head_norm(inner + cross, attn_gain)
    out_full = lax.all_gather(out_weight, "ctx", axis=0)
    return layer(
        attn_out,
        out_full,
        residual,
        expert_ids.T,
        ffn_gain.reshape(1, -1),
        router.T,
        w_gate[0].T,
        w_up[0].T,
        w_down[0],
    )


def solution(mesh):
    return jax.shard_map(
        per_device,
        mesh=mesh,
        in_specs=(
            P("ctx", "exp"),
            P("ctx", "exp"),
            P("ctx", "exp"),
            P("ctx", "exp"),
            P("exp"),
            P("exp", "ctx"),
            P(("ctx", "exp"), None),
            P(),
            P(),
            P("ctx", None),
            P("exp", None, "ctx"),
            P("exp", None, "ctx"),
            P("exp", "ctx", None),
        ),
        out_specs=P(("ctx", "exp"), None),
        check_vma=False,
    )
```

```python
import functools

import jax
import jax.numpy as jnp
from jax import lax
from jax.experimental import pallas as pl
from jax.experimental.pallas import tpu as pltpu
from jax.sharding import PartitionSpec as P

MESH = pl.DeviceIdType.MESH
F32 = jnp.float32
BF16 = jnp.bfloat16
EXPERTS = 16
CAP = 80
UNIT = 128
STAGES = 3
LINKS = 288


def place():
    ctx = lax.axis_index("ctx")
    exp = lax.axis_index("exp")
    return ctx // 2, ctx % 2, exp // 4, exp % 4


def along(axis, step):
    y, core, x, z = place()
    step = step % 4
    if axis == "x":
        return (y * 2 + core, (x + step) % 4 * 4 + z)
    if axis == "z":
        return (y * 2 + core, x * 4 + (z + step) % 4)
    return ((y + step) % 4 * 2 + core, x * 4 + z)


def exp_peer(step):
    return (lax.axis_index("ctx"), (lax.axis_index("exp") + step) % EXPERTS)


def ctx_peer(step):
    return ((lax.axis_index("ctx") + step) % 8, lax.axis_index("exp"))


def other_core():
    y, core, _, _ = place()
    return (y * 2 + 1 - core, lax.axis_index("exp"))


class Links:
    def __init__(self, send, recv):
        self.send, self.recv, self.count = send, recv, 0
        self.open, self.done = [], 0

    def copy(self, src, dst, device):
        made = pltpu.make_async_remote_copy(
            src_ref=src,
            dst_ref=dst,
            send_sem=self.send.at[self.count],
            recv_sem=self.recv.at[self.count],
            device_id=device,
            device_id_type=MESH,
        )
        made.start()
        self.count += 1
        assert self.count <= LINKS
        self.open.append(made)
        return made

    def drain(self, until=None):
        until = self.count if until is None else until
        for made in self.open[self.done : until]:
            made.wait_send()
        self.done = max(self.done, until)


def add_into(target, extra):
    size = 128 if target.shape[0] % 128 == 0 else 80

    def one(i, carry):
        rows = rows_at(i * size, size)
        target[rows, :] = (target[rows, :].astype(F32) + extra[rows, :].astype(F32)).astype(BF16)
        return carry

    lax.fori_loop(0, target.shape[0] // size, one, 0)


class RingSum:
    def __init__(self, links, axis, part, base, n, stride, first, second):
        place_of = dict(zip(("y", "core", "x", "z"), place()))
        self.links, self.axis, self.i = links, axis, place_of[axis]
        self.part, self.base, self.n, self.stride = part, base, n, stride
        self.first, self.second = first, second

    def low(self, d):
        return self.part.at[rows_at(self.base + d * self.stride, self.n // 2)]

    def high(self, d):
        return self.part.at[rows_at(self.base + d * self.stride + self.n // 2, self.n // 2)]

    def slot(self, k):
        return pl.ds(k * (self.n // 2), self.n // 2)

    def opposite(self):
        far, slot = (self.i + 2) % 4, self.slot
        up = self.links.copy(self.low(far), self.first.at[slot(0)], along(self.axis, 1))
        down = self.links.copy(self.high(far), self.first.at[slot(1)], along(self.axis, -1))
        self.far = (up, down)

    def direct_up(self):
        up, slot = (self.i + 1) % 4, self.slot
        self.near = [self.links.copy(self.high(up), self.second.at[slot(1)], along(self.axis, 1))]

    def direct_down(self):
        down, slot = (self.i + 3) % 4, self.slot
        self.near.append(
            self.links.copy(self.low(down), self.second.at[slot(2)], along(self.axis, -1))
        )

    def relay(self):
        up, down, slot = (self.i + 1) % 4, (self.i + 3) % 4, self.slot
        self.far[0].wait_recv()
        add_into(self.low(up), self.first.at[slot(0)])
        self.near.append(
            self.links.copy(self.low(up), self.second.at[slot(0)], along(self.axis, 1))
        )
        self.far[1].wait_recv()
        add_into(self.high(down), self.first.at[slot(1)])
        self.near.append(
            self.links.copy(self.high(down), self.second.at[slot(3)], along(self.axis, -1))
        )

    def arrived(self):
        for made in self.near:
            made.wait_recv()

    def total(self, start, size):
        own = self.part[rows_at(self.base + self.i * self.stride + start, size), :].astype(F32)
        own = own + self.second[rows_at(start, size), :].astype(F32)
        return own + self.second[rows_at(self.n + start, size), :].astype(F32)


def columns(start, size):
    return pl.ds(pl.multiple_of(start, 128), size)


def rows_at(start, size):
    return pl.ds(pl.multiple_of(start, 16), size)


def split3(value):
    one = value.astype(BF16)
    rest = value - one.astype(F32)
    two = rest.astype(BF16)
    return one, two, (rest - two.astype(F32)).astype(BF16)


def layer_kernel(
    query_ref,
    key_ref,
    value_ref,
    decay_ref,
    head_gain_ref,
    out_w_ref,
    resid_ref,
    ids_ref,
    gain_ref,
    router_ref,
    gate_ref,
    up_ref,
    down_ref,
    out_ref,
    state,
    chip_state,
    states,
    carried,
    gone,
    attn_ref,
    wide,
    gate_up,
    work,
    second,
    half,
    last_first,
    last_second,
    resid_parts,
    resid_cols,
    hidden,
    table,
    pieces,
    rows_in,
    tokens,
    scales,
    sums,
    active,
    partner,
    first_y,
    second_y,
    back,
    rows_out,
    local,
    send,
    recv,
    state_send,
    state_recv,
):
    y, core, x, z = place()
    ctx = y * 2 + core
    me = lax.axis_index("exp")
    links = Links(send, recv)
    above, below, far = (y + 1) % 4, (y + 3) % 4, (y + 2) % 4

    def chip_at(home, k):
        return (home + (0, 1, 3, 2)[k]) % 4

    def unit_cols(j):
        k = j // 12
        chip = (y + k + k // 2 - 2 * (k // 3)) % 4
        return columns(chip * 1536 + j % 12 * UNIT, UNIT)

    load_gate = pltpu.make_async_copy(gate_ref, gate_up.at[pl.ds(0, 576)], local.at[1])
    load_up = pltpu.make_async_copy(up_ref, gate_up.at[pl.ds(576, 576)], local.at[2])
    w_all, w_low, w_high = pl.ds(0, 512), pl.ds(0, 256), pl.ds(256, 256)

    def w_part(chip, side, rows):
        return wide.at[chip, rows, columns(side * 768, 768)]

    load_w = pltpu.make_async_copy(out_w_ref, w_part(y, core, w_all), local.at[0])
    load_w.start()

    barrier = pltpu.get_barrier_semaphore()
    for device in [along("y", 1), along("y", 3), other_core(), along("y", 2)]:
        pl.semaphore_signal(barrier, inc=1, device_id=device, device_id_type=MESH)
    for step in range(1, EXPERTS):
        pl.semaphore_signal(barrier, inc=1, device_id=exp_peer(step), device_id_type=MESH)

    earlier = lax.broadcasted_iota(jnp.int32, (512, 512), 1) <= lax.broadcasted_iota(
        jnp.int32, (512, 512), 0
    )
    lower = jnp.where(earlier, 1.0, 0.0).astype(BF16)
    turned = (((1,), (1,)), ((), ()))
    first = (((0,), (0,)), ((), ()))
    run_col = jnp.zeros((512, 4), F32)
    run_row = jnp.zeros((4, 512), F32)
    for term in split3(decay_ref[...]):
        run_col = run_col + lax.dot_general(lower, term, turned, preferred_element_type=F32)
        run_row = run_row + lax.dot_general(term, lower, turned, preferred_element_type=F32)
    lines = lax.broadcasted_iota(jnp.int32, (4, 128), 0)
    ends = jnp.zeros((4, 128), F32)
    for h in range(4):
        lanes = pl.ds(h * 128, 128)
        end = run_col[511:512, h : h + 1]
        to_end = jnp.exp(end - run_col[:, h : h + 1])
        decayed = (key_ref[:, lanes].astype(F32) * to_end).astype(BF16)
        own = lax.dot_general(decayed, value_ref[:, lanes], first, preferred_element_type=F32)
        state[pl.ds(h * 128, 128), :] = own.astype(BF16)
        ends = jnp.where(lines == h, end, ends)

    def pack_ends(value):
        parts = [t.astype(F32) for t in split3(value)]
        return jnp.concatenate(parts + [jnp.zeros((4, 128), F32)], axis=0).astype(BF16)

    def ends_of(ref):
        value = ref[pl.ds(512, 16), :].astype(F32)
        return value[0:4] + value[4:8] + value[8:12]

    state[pl.ds(512, 16), :] = pack_ends(ends)

    pl.semaphore_wait(barrier, EXPERTS + 3)

    def state_copy(src, dst, k, device):
        return pltpu.make_async_remote_copy(
            src_ref=src,
            dst_ref=dst,
            send_sem=state_send.at[k],
            recv_sem=state_recv.at[k],
            device_id=device,
            device_id_type=MESH,
        )

    def state_pair():
        return state_copy(state, states.at[0], 0, other_core())

    def state_up(step):
        return state_copy(chip_state, states.at[step], step, along("y", step))

    def state_over(step):
        return state_copy(states.at[step], states.at[step], 4 + step, other_core())

    @pl.when(core == 0)
    def _():
        state_pair().start()

    def spread_w(chip, side, rows, device, own=False):
        return links.copy(out_w_ref.at[rows] if own else w_part(chip, side, rows), w_part(chip, side, rows), device)

    w_up_low = spread_w(y, core, w_low, along("y", 1), True)
    w_down_high = spread_w(y, core, w_high, along("y", -1), True)
    w_pair = [spread_w(y, core, w_all, other_core(), True)]

    @pl.when(core == 1)
    def _():
        state_pair().wait_recv()
        own_ends = ends_of(state)
        for h in range(4):
            rows = pl.ds(h * 128, 128)
            joined = jnp.exp(own_ends[h : h + 1]) * states[0, rows, :].astype(F32)
            chip_state[rows, :] = (joined + state[rows, :].astype(F32)).astype(BF16)
        chip_state[pl.ds(512, 16), :] = pack_ends(own_ends + ends_of(states.at[0]))
        for step in range(1, 4):

            @pl.when(y + step < 4)
            def _(step=step):
                state_up(step).start()

    w_up_high = spread_w(y, core, w_high, along("y", 1), True)
    w_down_low = spread_w(y, core, w_low, along("y", -1), True)
    load_gate.start()
    load_up.start()

    def resid_part(g, carry):
        for s in range(STAGES):
            resid_parts[g, :, pl.ds(s * UNIT, UNIT)] = resid_ref[:, unit_cols(s * EXPERTS + g)]
        return carry

    lax.fori_loop(0, EXPERTS, resid_part, 0)
    resid_moves = []
    for step in range(1, EXPERTS):
        to = (me + step) % EXPERTS
        resid_moves.append(
            links.copy(resid_parts.at[to], resid_cols.at[rows_at(me * 32, 32)], exp_peer(step))
        )
    resid_cols[rows_at(me * 32, 32), :] = resid_parts[me]

    for h in range(4):
        lanes = pl.ds(h * 128, 128)
        for r in range(2):
            seen = (r + 1) * 256
            rows = pl.ds(r * 256, 256)
            scores = lax.dot_general(
                query_ref[rows, lanes],
                key_ref[pl.ds(0, seen), lanes],
                turned,
                preferred_element_type=F32,
            )
            spread_of = run_col[r * 256 : seen, h : h + 1] - run_row[h : h + 1, :seen]
            late = lax.broadcasted_iota(jnp.int32, (256, seen), 0) + r * 256
            soon = lax.broadcasted_iota(jnp.int32, (256, seen), 1)
            decay = jnp.where(late >= soon, jnp.exp(jnp.minimum(spread_of, 0.0)), 0.0)
            sums[rows, lanes] = jnp.dot(
                (scores * decay).astype(BF16),
                value_ref[pl.ds(0, seen), lanes],
                preferred_element_type=F32,
            )

    for step in range(1, 4):

        @pl.when((core == 1) & (y >= step))
        def _(step=step):
            state_up(step).wait_recv()
            state_over(step).start()

    w_up_low.wait_recv()
    w_on_up = spread_w(below, core, w_low, along("y", 1))
    w_pair.append(spread_w(below, core, w_low, other_core()))
    w_down_high.wait_recv()
    w_on_down = spread_w(above, core, w_high, along("y", -1))
    w_pair.append(spread_w(above, core, w_high, other_core()))

    experts = lax.broadcasted_iota(jnp.int32, (EXPERTS, 512), 0)
    picked = (ids_ref[0:1, :] == experts) | (ids_ref[1:2, :] == experts)
    before = lax.broadcasted_iota(jnp.int32, (512, 512), 0) < lax.broadcasted_iota(
        jnp.int32, (512, 512), 1
    )
    rank = jnp.dot(
        jnp.where(picked, 1.0, 0.0).astype(BF16),
        jnp.where(before, 1.0, 0.0).astype(BF16),
        preferred_element_type=F32,
    )
    code = jnp.where(picked, rank, -1.0)
    slots = lax.broadcasted_iota(jnp.int32, (CAP, 512), 0).astype(F32)
    for e in range(EXPERTS):
        table[pl.ds(e * CAP, CAP), :] = jnp.where(code[e : e + 1, :] == slots, 1.0, 0.0).astype(
            BF16
        )

    carried[...] = jnp.zeros((512, 128), F32)
    gone[...] = jnp.zeros((4, 128), F32)
    for step in range(1, 4):

        @pl.when((core == 0) & (y >= step))
        def _(step=step):
            state_over(step).wait_recv()

        @pl.when(y >= step)
        def _(step=step):
            for h in range(4):
                rows = pl.ds(h * 128, 128)
                kept = jnp.exp(gone[pl.ds(h, 1), :])
                carried[rows, :] = carried[rows, :] + kept * states[step, rows, :].astype(F32)
            gone[...] = gone[...] + ends_of(states.at[step])

    @pl.when(core == 1)
    def _():
        pair_ends = ends_of(states.at[0])
        for h in range(4):
            rows = pl.ds(h * 128, 128)
            kept = jnp.exp(pair_ends[h : h + 1])
            carried[rows, :] = kept * carried[rows, :] + states[0, rows, :].astype(F32)

    for h in range(4):
        lanes = pl.ds(h * 128, 128)
        full = carried[lanes, :]
        near = full.astype(BF16)
        rest = (full - near.astype(F32)).astype(BF16)
        asked = query_ref[:, lanes]
        cross = jnp.dot(asked, near, preferred_element_type=F32)
        cross = cross + jnp.dot(asked, rest, preferred_element_type=F32)
        total = sums[pl.ds(0, 512), lanes] + jnp.exp(run_col[:, h : h + 1]) * cross
        mean = jnp.mean(total * total, axis=1, keepdims=True)
        attn_ref[:, lanes] = (
            total * lax.rsqrt(mean + 1e-06) * head_gain_ref[:, lanes]
        ).astype(BF16)

    w_up_high.wait_recv()
    w_pair.append(spread_w(below, core, w_high, other_core()))
    w_down_low.wait_recv()
    w_pair.append(spread_w(above, core, w_low, other_core()))
    load_w.wait()
    for made in w_pair:
        made.wait_recv()

    rings_a, rings_b, lasts_a, lasts_b = [], [], [], []
    for s in range(STAGES):
        for which, (rings, axis) in enumerate(((rings_a, "x"), (rings_b, "z"))):
            k = which * STAGES + s
            rings.append(
                RingSum(
                    links,
                    axis,
                    work,
                    k * 4096,
                    1024,
                    1024,
                    work.at[pl.ds(6 * 4096 + k * 1024, 1024)],
                    second.at[pl.ds(k * 2048, 2048)],
                )
            )
        for which, (rings, axis) in enumerate(((lasts_a, "z"), (lasts_b, "x"))):
            k = which * STAGES + s
            rings.append(
                RingSum(
                    links,
                    axis,
                    half,
                    k * 1024,
                    256,
                    256,
                    last_first.at[pl.ds(k * 256, 256)],
                    last_second.at[pl.ds(k * 512, 512)],
                )
            )

    def project_quad(s, to):
        quad = s * 4 + to
        k = quad // 3
        chip = (y + k + k // 2 - 2 * (k // 3)) % 4
        w = wide[chip, pl.ds(0, 512), columns(quad % 3 * 512, 512)]
        r = jnp.dot(attn_ref[...], w, preferred_element_type=F32).astype(BF16)
        for u in range(4):
            for side in range(2):
                start = s * 4096 + to * 1024 + (side * 4 + u) * 128
                work[rows_at(start, 128), :] = r[
                    side * 128 : side * 128 + 128, u * UNIT : u * UNIT + UNIT
                ]
                start = (STAGES + s) * 4096 + u * 1024 + (side * 4 + to) * 128
                work[rows_at(start, 128), :] = r[
                    256 + side * 128 : 256 + side * 128 + 128, u * UNIT : u * UNIT + UNIT
                ]

    def project(s):
        def one(i, carry):
            project_quad(s, (x + 3 + i) % 4)
            return carry

        project_quad(s, (x + 2) % 4)
        rings_a[s].opposite()
        lax.fori_loop(0, 3, one, 0)
        rings_b[s].opposite()
        rings_a[s].direct_up()
        rings_a[s].direct_down()
        rings_b[s].direct_up()
        rings_b[s].direct_down()

    def relay(s):
        rings_a[s].relay()
        rings_b[s].relay()

    def turn(s):
        for ring, last in ((rings_a[s], lasts_a[s]), (rings_b[s], lasts_b[s])):
            ring.arrived()

            def one(u, carry, ring=ring, last=last):
                for side in range(2):
                    rows = rows_at(last.base + u * 256 + side * 128, 128)
                    half[rows, :] = ring.total(side * 512 + u * 128, 128).astype(BF16)
                return carry

            lax.fori_loop(0, 4, one, 0)
            last.opposite()
            last.direct_up()
            last.direct_down()

    def turn_relay(s):
        lasts_a[s].relay()
        lasts_b[s].relay()

    row_moves = [[] for _ in range(STAGES)]

    def dispatch(s):
        cols = pl.ds(s * UNIT, UNIT)
        if s == 0:
            for made in resid_moves:
                made.wait_recv()
        for start, ring in ((0, lasts_a[s]), (256, lasts_b[s])):
            ring.arrived()
            rows = pl.ds(start, 256)
            hidden[rows, cols] = (
                ring.total(0, 256) + resid_cols[rows, cols].astype(F32)
            ).astype(BF16)
        found = jnp.dot(table[...], hidden[:, cols], preferred_element_type=F32)
        pieces[pl.ds(s * EXPERTS * CAP, EXPERTS * CAP), :] = found.astype(BF16)
        lands = rows_in.at[:, columns((s * EXPERTS + me) * UNIT, UNIT)]
        for step in range(1, EXPERTS):
            to = (me + step) % EXPERTS
            piece = pieces.at[rows_at((s * EXPERTS + to) * CAP, CAP)]
            row_moves[s].append(links.copy(piece, lands, exp_peer(step)))
        lands[...] = pieces[rows_at((s * EXPERTS + me) * CAP, CAP), :]

    squares = [jnp.zeros((CAP, 1), F32)]
    mine = rows_at(ctx * CAP, CAP)
    gathers = [None] * STAGES

    def spread(s, block, side, device):
        cols = pl.ds(s * 2048 + side * 1024, 1024)
        if side == 2:
            cols = pl.ds(s * 2048, 2048)
        ref = tokens.at[rows_at(block * CAP, CAP), cols]
        return links.copy(ref, ref, device)

    def gather(s):
        for made in row_moves[s]:
            made.wait_recv()
        for u in range(EXPERTS):
            cols = pl.ds((s * EXPERTS + u) * UNIT, UNIT)
            part = rows_in[:, cols].astype(F32)
            squares[0] = squares[0] + jnp.sum(part * part, axis=1, keepdims=True)
            tokens[mine, cols] = (part * gain_ref[:, unit_cols(s * EXPERTS + u)]).astype(BF16)
        gathers[s] = dict(
            up_low=spread(s, ctx, 0, along("y", 1)),
            down_high=spread(s, ctx, 1, along("y", -1)),
            up_high=spread(s, ctx, 1, along("y", 1)),
            down_low=spread(s, ctx, 0, along("y", -1)),
            pair=[spread(s, ctx, 2, other_core())],
        )

    from_below, from_above, from_far = below * 2 + core, above * 2 + core, far * 2 + core

    def gather_mid(s):
        g = gathers[s]
        g["up_low"].wait_recv()
        g["on_up"] = spread(s, from_below, 0, along("y", 1))
        g["near"] = [spread(s, from_below, 0, other_core())]
        g["down_high"].wait_recv()
        g["on_down"] = spread(s, from_above, 1, along("y", -1))
        g["near"].append(spread(s, from_above, 1, other_core()))

    def gather_near(s):
        g = gathers[s]
        g["up_high"].wait_recv()
        g["near"].append(spread(s, from_below, 1, other_core()))
        g["down_low"].wait_recv()
        g["near"].append(spread(s, from_above, 0, other_core()))

    def gather_far(s):
        g = gathers[s]
        g["on_up"].wait_recv()
        g["far"] = [spread(s, from_far, 0, other_core())]
        g["on_down"].wait_recv()
        g["far"].append(spread(s, from_far, 1, other_core()))

    def held(s, names):
        for name in names:
            for made in gathers[s][name]:
                made.wait_recv()

    def gate_and_up(s, chip):
        rows = rows_at(chip * (2 * CAP), 2 * CAP)
        total = None
        quad = s * 4
        while quad < s * 4 + 4:
            run = min(3 - quad % 3, s * 4 + 4 - quad)
            start = columns(chip_at(chip, quad // 3) * 1536 + quad % 3 * 512, run * 512)
            part = lax.dot_general(
                tokens[rows, pl.ds(quad * 512, run * 512)],
                gate_up[:, start],
                turned,
                preferred_element_type=F32,
            )
            total = part if total is None else total + part
            quad += run
        if s > 0:
            total = total + sums[rows, :]
        if s < STAGES - 1:
            sums[rows, :] = total
            return
        total = total * scales[rows, 0:1]
        gate, upper = total[:, :576], total[:, 576:]
        active[...] = (gate / (1.0 + jnp.exp(-gate)) * upper).astype(BF16)

    def gate_and_up_all(s):
        def one(chip, carry):
            gate_and_up(s, chip)
            return carry

        lax.fori_loop(0, 4, one, 0)

    project(0)
    relay(0)
    project(1)
    turn(0)
    w_on_up.wait_recv()
    w_pair_far = [spread_w(far, core, w_low, other_core())]
    w_on_down.wait_recv()
    w_pair_far.append(spread_w(far, core, w_high, other_core()))
    relay(1)
    turn_relay(0)
    for made in w_pair_far:
        made.wait_recv()
    project(2)
    dispatch(0)
    turn(1)
    relay(2)
    turn_relay(1)
    gather(0)
    dispatch(1)
    turn(2)
    gather_mid(0)
    turn_relay(2)
    gather(1)
    gather_near(0)
    dispatch(2)
    sent_rows = links.count
    gather_far(0)
    gather_mid(1)
    links.drain(sent_rows)
    load_down = []
    for k in range(4):
        made = pltpu.make_async_copy(
            down_ref.at[:, pl.ds(k * 1536, 1536)], wide.at[k], local.at[3 + k]
        )
        made.start()
        load_down.append(made)
    load_gate.wait()
    load_up.wait()
    held(0, ("pair", "near", "far"))
    gather(2)

    def spread_scale(block, device):
        ref = scales.at[rows_at(block * CAP, CAP)]
        return links.copy(ref, ref, device)

    scale = lax.rsqrt(squares[0] / 6144.0 + 1e-05)
    scales[mine, :] = jnp.broadcast_to(scale, (CAP, UNIT))
    scale_up = spread_scale(ctx, along("y", 1))
    scale_down = spread_scale(ctx, along("y", -1))
    scale_pair = [spread_scale(ctx, other_core())]
    gather_near(1)
    gather_far(1)
    gate_and_up_all(0)
    gather_mid(2)
    scale_up.wait_recv()
    scale_on = spread_scale(from_below, along("y", 1))
    scale_pair.append(spread_scale(from_below, other_core()))
    scale_down.wait_recv()
    scale_pair.append(spread_scale(from_above, other_core()))
    held(1, ("pair", "near", "far"))
    gate_and_up_all(1)
    gather_near(2)
    scale_on.wait_recv()
    scale_pair.append(spread_scale(from_far, other_core()))

    my_ids = lax.dot_general(
        table[rows_at(me * CAP, CAP), :],
        ids_ref[...].astype(F32).astype(BF16),
        turned,
        preferred_element_type=F32,
    )
    logits = jnp.zeros((CAP, EXPERTS), F32)
    for k in range(4):
        part = router_ref[:, columns(chip_at(y, k) * 1536, 1536)]
        router_high = part.astype(BF16)
        router_low = (part - router_high.astype(F32)).astype(BF16)
        token = tokens[mine, pl.ds(k * 1536, 1536)]
        for w in (router_high, router_low):
            logits = logits + lax.dot_general(token, w, turned, preferred_element_type=F32)
    gates = 1.0 / (1.0 + jnp.exp(-logits * scale))
    lanes = lax.broadcasted_iota(jnp.int32, (CAP, EXPERTS), 1)
    lanes_f = lanes.astype(F32)
    both = (my_ids[:, 0:1] == lanes_f) | (my_ids[:, 1:2] == lanes_f)
    total = jnp.sum(jnp.where(both, gates, 0.0), axis=1, keepdims=True)
    share = jnp.sum(jnp.where(lanes == me, gates, 0.0), axis=1, keepdims=True) / total

    block = EXPERTS * CAP
    for made in load_down:
        made.wait()

    def down(chip):
        def one(quad, carry):
            k = quad // 3
            part = (chip + k + k // 2 - 2 * (k // 3)) % 4
            w = wide[part, :, columns(quad % 3 * 512, 512)]
            o = jnp.dot(active[...], w, preferred_element_type=F32).astype(BF16)
            for owner in range(2):
                for u in range(4):
                    start = (owner * 4 + chip) * (STAGES * block) + (quad * 4 + u) * CAP
                    work[rows_at(start, CAP), :] = o[
                        owner * CAP : owner * CAP + CAP, u * UNIT : u * UNIT + UNIT
                    ]
            return carry

        lax.fori_loop(0, 4 * STAGES, one, 0)
        return links.copy(
            work.at[rows_at(((1 - core) * 4 + chip) * (STAGES * block), STAGES * block)],
            partner.at[rows_at(chip * (STAGES * block), STAGES * block)],
            other_core(),
        )

    def join(chip, made):
        made.wait_recv()
        add_into(
            work.at[rows_at((core * 4 + chip) * (STAGES * block), STAGES * block)],
            partner.at[rows_at(chip * (STAGES * block), STAGES * block)],
        )

    rings_y = [
        RingSum(
            links,
            "y",
            work,
            core * (4 * STAGES * block) + s * block,
            block,
            STAGES * block,
            first_y.at[pl.ds(s * block, block)],
            second_y.at[pl.ds(s * 2 * block, 2 * block)],
        )
        for s in range(STAGES)
    ]
    held(2, ("pair", "near"))
    for made in scale_pair:
        made.wait_recv()
    gate_and_up(2, above)
    sum_above = down(above)
    gate_and_up(2, below)
    gather_far(2)
    sum_below = down(below)
    join(above, sum_above)
    for ring in rings_y:
        ring.direct_up()
    held(2, ("far",))
    gate_and_up(2, far)
    sum_far = down(far)
    join(below, sum_below)
    for ring in rings_y:
        ring.direct_down()
    gate_and_up(2, y)
    join(far, sum_far)
    for ring in rings_y:
        ring.opposite()
    sum_own = down(y)
    join(y, sum_own)

    back_moves = []

    def give_back(s):
        rings_y[s].arrived()

        def one(g, carry):
            total = rings_y[s].total(g * CAP, CAP).astype(BF16).astype(F32)
            pieces[rows_at((s * EXPERTS + g) * CAP, CAP), :] = (total * share).astype(BF16)
            return carry

        lax.fori_loop(0, EXPERTS, one, 0)
        lands = back.at[rows_at(me * CAP, CAP), pl.ds(s * UNIT, UNIT)]
        for step in range(1, EXPERTS):
            to = (me + step) % EXPERTS
            piece = pieces.at[rows_at((s * EXPERTS + to) * CAP, CAP)]
            back_moves.append(links.copy(piece, lands, exp_peer(step)))
        lands[...] = pieces[rows_at((s * EXPERTS + me) * CAP, CAP), :]

    rings_y[0].relay()
    rings_y[1].relay()
    rings_y[2].relay()
    give_back(0)
    give_back(1)
    give_back(2)
    for made in back_moves:
        made.wait_recv()
    summed = lax.dot_general(table[...], back[...], first, preferred_element_type=F32)
    hidden[...] = (hidden[...].astype(F32) + summed).astype(BF16)

    out_moves = []
    for step in range(1, EXPERTS):
        to = (me + step) % EXPERTS
        out_moves.append(
            links.copy(hidden.at[rows_at(to * 32, 32)], rows_out.at[me], exp_peer(step))
        )
    rows_out[me] = hidden[rows_at(me * 32, 32), :]
    for made in out_moves:
        made.wait_recv()

    def put(g, carry):
        for s in range(STAGES):
            out_ref[:, unit_cols(s * EXPERTS + g)] = rows_out[g, :, pl.ds(s * UNIT, UNIT)]
        return carry

    lax.fori_loop(0, EXPERTS, put, 0)
    links.drain()

    @pl.when(core == 0)
    def _():
        state_pair().wait_send()

    for step in range(1, 4):

        @pl.when((core == 1) & (y + step < 4))
        def _(step=step):
            state_up(step).wait_send()

        @pl.when((core == 1) & (y >= step))
        def _(step=step):
            state_over(step).wait_send()


def layer(*arrays):
    vmem = pl.BlockSpec(memory_space=pltpu.VMEM)
    hbm = pl.BlockSpec(memory_space=pl.ANY)

    def rows(n, width=UNIT):
        return pltpu.VMEM((n, width), BF16)

    block = EXPERTS * CAP
    return pl.pallas_call(
        layer_kernel,
        out_shape=jax.ShapeDtypeStruct((32, 6144), BF16),
        in_specs=[vmem] * 5 + [hbm, vmem, vmem, vmem, vmem, hbm, hbm, hbm],
        out_specs=vmem,
        scratch_shapes=[
            rows(528),
            rows(528),
            pltpu.VMEM((4, 528, 128), BF16),
            pltpu.VMEM((512, 128), F32),
            pltpu.VMEM((4, 128), F32),
            rows(512, 512),
            pltpu.VMEM((4, 576, 1536), BF16),
            rows(1152, 6144),
            rows(24 * block),
            rows(6 * 2048),
            rows(6 * 1024),
            rows(6 * 256),
            rows(6 * 512),
            pltpu.VMEM((EXPERTS, 32, STAGES * UNIT), BF16),
            rows(512, STAGES * UNIT),
            rows(512, STAGES * UNIT),
            rows(block, 512),
            rows(STAGES * block),
            rows(CAP, 6144),
            rows(8 * CAP, 6144),
            pltpu.VMEM((8 * CAP, UNIT), F32),
            pltpu.VMEM((8 * CAP, 1152), F32),
            rows(2 * CAP, 576),
            rows(4 * STAGES * block),
            rows(STAGES * block),
            rows(2 * STAGES * block),
            rows(block, STAGES * UNIT),
            pltpu.VMEM((EXPERTS, 32, STAGES * UNIT), BF16),
            pltpu.SemaphoreType.DMA((7,)),
            pltpu.SemaphoreType.DMA((LINKS,)),
            pltpu.SemaphoreType.DMA((LINKS,)),
            pltpu.SemaphoreType.DMA((8,)),
            pltpu.SemaphoreType.DMA((8,)),
        ],
        compiler_params=pltpu.CompilerParams(
            collective_id=0, has_side_effects=True, vmem_limit_bytes=65000 << 10
        ),
        name="layer",
    )(*arrays)


def per_device(
    query_rows,
    key_rows,
    value_rows,
    log_decay,
    attn_gain,
    out_weight,
    residual,
    ffn_gain,
    router,
    expert_ids,
    w_gate,
    w_up,
    w_down,
):
    return layer(
        query_rows,
        key_rows,
        value_rows,
        log_decay.T,
        attn_gain.reshape(1, -1),
        out_weight,
        residual,
        expert_ids.T,
        ffn_gain.reshape(1, -1),
        router.T,
        w_gate[0].T,
        w_up[0].T,
        w_down[0],
    )


def solution(mesh):
    return jax.shard_map(
        per_device,
        mesh=mesh,
        in_specs=(
            P("ctx", "exp"),
            P("ctx", "exp"),
            P("ctx", "exp"),
            P("ctx", "exp"),
            P("exp"),
            P("exp", "ctx"),
            P(("ctx", "exp"), None),
            P(),
            P(),
            P("ctx", None),
            P("exp", None, "ctx"),
            P("exp", None, "ctx"),
            P("exp", "ctx", None),
        ),
        out_specs=P(("ctx", "exp"), None),
        check_vma=False,
    )
```

```python
import functools

import jax
import jax.numpy as jnp
from jax import lax
from jax.experimental import pallas as pl
from jax.experimental.pallas import tpu as pltpu
from jax.sharding import PartitionSpec as P

MESH = pl.DeviceIdType.MESH
F32 = jnp.float32
BF16 = jnp.bfloat16
EXPERTS = 16
CAP = 80
UNIT = 128
STAGES = 3
LINKS = 304


def place():
    ctx = lax.axis_index("ctx")
    exp = lax.axis_index("exp")
    return ctx // 2, ctx % 2, exp // 4, exp % 4


def along(axis, step):
    y, core, x, z = place()
    step = step % 4
    if axis == "x":
        return (y * 2 + core, (x + step) % 4 * 4 + z)
    if axis == "z":
        return (y * 2 + core, x * 4 + (z + step) % 4)
    return ((y + step) % 4 * 2 + core, x * 4 + z)


def exp_peer(step):
    return (lax.axis_index("ctx"), (lax.axis_index("exp") + step) % EXPERTS)


def ctx_peer(step):
    return ((lax.axis_index("ctx") + step) % 8, lax.axis_index("exp"))


def other_core():
    y, core, _, _ = place()
    return (y * 2 + 1 - core, lax.axis_index("exp"))


class Links:
    def __init__(self, send, recv):
        self.send, self.recv, self.count = send, recv, 0
        self.open, self.group, self.early = {}, "w", None

    def copy(self, src, dst, device):
        made = pltpu.make_async_remote_copy(
            src_ref=src,
            dst_ref=dst,
            send_sem=self.send.at[self.count],
            recv_sem=self.recv.at[self.count],
            device_id=device,
            device_id_type=MESH,
        )
        made.start()
        self.count += 1
        assert self.count <= LINKS
        self.open.setdefault(self.group, []).append(made)
        return made

    def drain(self, group):
        for made in self.open.pop(group, []):
            if made is not self.early:
                made.wait_send()


def add_into(target, extra):
    size = 128 if target.shape[0] % 128 == 0 else 80

    def one(i, carry):
        rows = rows_at(i * size, size)
        target[rows, :] = (target[rows, :].astype(F32) + extra[rows, :].astype(F32)).astype(BF16)
        return carry

    lax.fori_loop(0, target.shape[0] // size, one, 0)


class RingSum:
    def __init__(self, links, axis, part, base, n, stride, first, second):
        place_of = dict(zip(("y", "core", "x", "z"), place()))
        self.links, self.axis, self.i = links, axis, place_of[axis]
        self.part, self.base, self.n, self.stride = part, base, n, stride
        self.first, self.second = first, second

    def low(self, d):
        return self.part.at[rows_at(self.base + d * self.stride, self.n // 2)]

    def high(self, d):
        return self.part.at[rows_at(self.base + d * self.stride + self.n // 2, self.n // 2)]

    def slot(self, k):
        return pl.ds(k * (self.n // 2), self.n // 2)

    def opposite(self):
        far, slot = (self.i + 2) % 4, self.slot
        up = self.links.copy(self.low(far), self.first.at[slot(0)], along(self.axis, 1))
        down = self.links.copy(self.high(far), self.first.at[slot(1)], along(self.axis, -1))
        self.far = (up, down)

    def direct_up(self):
        up, slot = (self.i + 1) % 4, self.slot
        self.near = [self.links.copy(self.high(up), self.second.at[slot(1)], along(self.axis, 1))]

    def direct_down(self):
        down, slot = (self.i + 3) % 4, self.slot
        self.near.append(
            self.links.copy(self.low(down), self.second.at[slot(2)], along(self.axis, -1))
        )

    def relay(self):
        up, down, slot = (self.i + 1) % 4, (self.i + 3) % 4, self.slot
        self.far[0].wait_recv()
        add_into(self.low(up), self.first.at[slot(0)])
        self.near.append(
            self.links.copy(self.low(up), self.second.at[slot(0)], along(self.axis, 1))
        )
        self.far[1].wait_recv()
        add_into(self.high(down), self.first.at[slot(1)])
        self.near.append(
            self.links.copy(self.high(down), self.second.at[slot(3)], along(self.axis, -1))
        )

    def arrived(self):
        for made in self.near:
            made.wait_recv()

    def total(self, start, size):
        own = self.part[rows_at(self.base + self.i * self.stride + start, size), :].astype(F32)
        own = own + self.second[rows_at(start, size), :].astype(F32)
        return own + self.second[rows_at(self.n + start, size), :].astype(F32)


class DirectSum:
    def __init__(self, links, axis, part, base, n, landed):
        place_of = dict(zip(("y", "core", "x", "z"), place()))
        self.links, self.axis, self.i = links, axis, place_of[axis]
        self.part, self.base, self.n, self.landed = part, base, n, landed

    def send(self):
        self.moves = [
            self.links.copy(
                self.part.at[rows_at(self.base + (self.i + step) % 4 * self.n, self.n)],
                self.landed.at[pl.ds((step - 1) * self.n, self.n)],
                along(self.axis, step),
            )
            for step in (2, 1, 3)
        ]

    def total(self):
        for made in self.moves:
            made.wait_recv()
        total = self.part[rows_at(self.base + self.i * self.n, self.n), :].astype(F32)
        for k in range(3):
            total = total + self.landed[pl.ds(k * self.n, self.n), :].astype(F32)
        return total


def columns(start, size):
    return pl.ds(pl.multiple_of(start, 128), size)


def rows_at(start, size):
    return pl.ds(pl.multiple_of(start, 16), size)


def split3(value):
    one = value.astype(BF16)
    rest = value - one.astype(F32)
    two = rest.astype(BF16)
    return one, two, (rest - two.astype(F32)).astype(BF16)


def layer_kernel(
    query_ref,
    key_ref,
    value_ref,
    decay_ref,
    head_gain_ref,
    out_w_ref,
    resid_ref,
    ids_ref,
    gain_ref,
    router_ref,
    gate_ref,
    up_ref,
    down_ref,
    out_ref,
    query,
    key,
    value,
    resid,
    routes,
    state,
    chip_state,
    states,
    carried,
    gone,
    attn_ref,
    wide,
    gate_up,
    work,
    second,
    half,
    last,
    resid_parts,
    resid_cols,
    hidden,
    table,
    pieces,
    rows_in,
    tokens,
    scales,
    sums,
    active,
    partner,
    first_y,
    second_y,
    back,
    rows_out,
    local,
    send,
    recv,
    state_send,
    state_recv,
):
    y, core, x, z = place()
    ctx = y * 2 + core
    me = lax.axis_index("exp")
    links = Links(send, recv)
    above, below, far = (y + 1) % 4, (y + 3) % 4, (y + 2) % 4

    def chip_at(home, k):
        return (home + (0, 1, 3, 2)[k]) % 4

    def unit_cols(j):
        k = j // 12
        chip = (y + k + k // 2 - 2 * (k // 3)) % 4
        return columns(chip * 1536 + j % 12 * UNIT, UNIT)

    barrier = pltpu.get_barrier_semaphore()
    for device in [along("y", 1), along("y", 3), other_core(), along("y", 2)]:
        pl.semaphore_signal(barrier, inc=1, device_id=device, device_id_type=MESH)
    for step in range(1, EXPERTS):
        pl.semaphore_signal(barrier, inc=1, device_id=exp_peer(step), device_id_type=MESH)

    load_gate = pltpu.make_async_copy(gate_ref, gate_up.at[pl.ds(0, 576)], local.at[1])
    load_up = pltpu.make_async_copy(up_ref, gate_up.at[pl.ds(576, 576)], local.at[2])
    w_all, w_low, w_high = pl.ds(0, 512), pl.ds(0, 256), pl.ds(256, 256)
    one_way, other_way = (2 * core + 3) % 4, (2 * core + 1) % 4
    one_chip, other_chip = (y + one_way) % 4, (y + other_way) % 4

    def w_part(chip, side, rows):
        return wide.at[chip, rows, columns(side * 768, 768)]

    load_in = []
    for k, (src, dst) in enumerate(
        (
            (key_ref, key),
            (value_ref, value),
            (query_ref, query),
            (resid_ref, resid),
            (router_ref, routes),
        )
    ):
        made = pltpu.make_async_copy(src, dst, local.at[7 + k])
        made.start()
        load_in.append(made)
    load_w = pltpu.make_async_copy(out_w_ref, w_part(y, core, w_all), local.at[0])
    load_w.start()

    earlier = lax.broadcasted_iota(jnp.int32, (512, 512), 1) <= lax.broadcasted_iota(
        jnp.int32, (512, 512), 0
    )
    lower = jnp.where(earlier, 1.0, 0.0).astype(BF16)
    turned = (((1,), (1,)), ((), ()))
    first = (((0,), (0,)), ((), ()))
    run_col = jnp.zeros((512, 4), F32)
    run_row = jnp.zeros((4, 512), F32)
    for term in split3(decay_ref[...]):
        run_col = run_col + lax.dot_general(lower, term, turned, preferred_element_type=F32)
        run_row = run_row + lax.dot_general(term, lower, turned, preferred_element_type=F32)
    load_in[0].wait()
    load_in[1].wait()
    lines = lax.broadcasted_iota(jnp.int32, (4, 128), 0)
    ends = jnp.zeros((4, 128), F32)
    for h in range(4):
        lanes = pl.ds(h * 128, 128)
        end = run_col[511:512, h : h + 1]
        to_end = jnp.exp(end - run_col[:, h : h + 1])
        decayed = (key[:, lanes].astype(F32) * to_end).astype(BF16)
        own = lax.dot_general(decayed, value[:, lanes], first, preferred_element_type=F32)
        state[pl.ds(h * 128, 128), :] = own.astype(BF16)
        ends = jnp.where(lines == h, end, ends)

    def pack_ends(value):
        parts = [t.astype(F32) for t in split3(value)]
        return jnp.concatenate(parts + [jnp.zeros((4, 128), F32)], axis=0).astype(BF16)

    def ends_of(ref):
        value = ref[pl.ds(512, 16), :].astype(F32)
        return value[0:4] + value[4:8] + value[8:12]

    state[pl.ds(512, 16), :] = pack_ends(ends)

    pl.semaphore_wait(barrier, EXPERTS + 3)

    def state_copy(src, dst, k, device):
        return pltpu.make_async_remote_copy(
            src_ref=src,
            dst_ref=dst,
            send_sem=state_send.at[k],
            recv_sem=state_recv.at[k],
            device_id=device,
            device_id_type=MESH,
        )

    def state_pair():
        return state_copy(state, states.at[0], 0, other_core())

    def state_up(step):
        return state_copy(chip_state, states.at[step], step, along("y", step))

    def state_over(step):
        return state_copy(states.at[step], states.at[step], 4 + step, other_core())

    state_pair().start()

    def spread_w(chip, rows, device):
        src = out_w_ref if chip is None else w_part(chip, core, rows)
        return links.copy(src, w_part(y if chip is None else chip, core, rows), device)

    w_first = spread_w(None, w_all, along("y", one_way))
    w_pair = [spread_w(None, w_all, other_core())]

    state_pair().wait_recv()

    @pl.when(core == 0)
    def _():
        pair_ends = ends_of(states.at[0])
        for h in range(4):
            rows = pl.ds(h * 128, 128)
            joined = jnp.exp(pair_ends[h : h + 1]) * state[rows, :].astype(F32)
            chip_state[rows, :] = (joined + states[0, rows, :].astype(F32)).astype(BF16)
        chip_state[pl.ds(512, 16), :] = pack_ends(pair_ends + ends_of(state))
        for step in range(1, 4):

            @pl.when(y + step < 4)
            def _(step=step):
                state_up(step).start()

    load_gate.start()
    load_up.start()

    for made in load_in[2:]:
        made.wait()

    def resid_part(g, carry):
        for s in range(STAGES):
            resid_parts[g, :, pl.ds(s * UNIT, UNIT)] = resid[:, unit_cols(s * EXPERTS + g)]
        return carry

    lax.fori_loop(0, EXPERTS, resid_part, 0)
    resid_moves = []
    links.group = "rows"
    for step in range(1, EXPERTS):
        to = (me + step) % EXPERTS
        resid_moves.append(
            links.copy(resid_parts.at[to], resid_cols.at[rows_at(me * 32, 32)], exp_peer(step))
        )
    resid_cols[rows_at(me * 32, 32), :] = resid_parts[me]

    for h in range(4):
        lanes = pl.ds(h * 128, 128)
        for r in range(2):
            seen = (r + 1) * 256
            rows = pl.ds(r * 256, 256)
            scores = lax.dot_general(
                query[rows, lanes],
                key[pl.ds(0, seen), lanes],
                turned,
                preferred_element_type=F32,
            )
            spread_of = run_col[r * 256 : seen, h : h + 1] - run_row[h : h + 1, :seen]
            late = lax.broadcasted_iota(jnp.int32, (256, seen), 0) + r * 256
            soon = lax.broadcasted_iota(jnp.int32, (256, seen), 1)
            decay = jnp.where(late >= soon, jnp.exp(jnp.minimum(spread_of, 0.0)), 0.0)
            sums[rows, lanes] = jnp.dot(
                (scores * decay).astype(BF16),
                value[pl.ds(0, seen), lanes],
                preferred_element_type=F32,
            )

    for step in range(1, 4):

        @pl.when((core == 0) & (y >= step))
        def _(step=step):
            state_up(step).wait_recv()
            state_over(step).start()

    links.group = "w"
    w_first.wait_send()
    links.early = w_first
    w_second = spread_w(None, w_all, along("y", other_way))
    w_first.wait_recv()
    w_near = spread_w(other_chip, w_all, other_core())
    w_far = [spread_w(other_chip, w_low, along("y", one_way))]

    experts = lax.broadcasted_iota(jnp.int32, (EXPERTS, 512), 0)
    picked = (ids_ref[0:1, :] == experts) | (ids_ref[1:2, :] == experts)
    before = lax.broadcasted_iota(jnp.int32, (512, 512), 0) < lax.broadcasted_iota(
        jnp.int32, (512, 512), 1
    )
    rank = jnp.dot(
        jnp.where(picked, 1.0, 0.0).astype(BF16),
        jnp.where(before, 1.0, 0.0).astype(BF16),
        preferred_element_type=F32,
    )
    code = jnp.where(picked, rank, -1.0)
    slots = lax.broadcasted_iota(jnp.int32, (CAP, 512), 0).astype(F32)
    for e in range(EXPERTS):
        table[pl.ds(e * CAP, CAP), :] = jnp.where(code[e : e + 1, :] == slots, 1.0, 0.0).astype(
            BF16
        )

    carried[...] = jnp.zeros((512, 128), F32)
    gone[...] = jnp.zeros((4, 128), F32)
    for step in range(1, 4):

        @pl.when((core == 1) & (y >= step))
        def _(step=step):
            state_over(step).wait_recv()

        @pl.when(y >= step)
        def _(step=step):
            for h in range(4):
                rows = pl.ds(h * 128, 128)
                kept = jnp.exp(gone[pl.ds(h, 1), :])
                carried[rows, :] = carried[rows, :] + kept * states[step, rows, :].astype(F32)
            gone[...] = gone[...] + ends_of(states.at[step])

    @pl.when(core == 1)
    def _():
        pair_ends = ends_of(states.at[0])
        for h in range(4):
            rows = pl.ds(h * 128, 128)
            kept = jnp.exp(pair_ends[h : h + 1])
            carried[rows, :] = kept * carried[rows, :] + states[0, rows, :].astype(F32)

    for h in range(4):
        lanes = pl.ds(h * 128, 128)
        full = carried[lanes, :]
        near = full.astype(BF16)
        rest = (full - near.astype(F32)).astype(BF16)
        asked = query[:, lanes]
        cross = jnp.dot(asked, near, preferred_element_type=F32)
        cross = cross + jnp.dot(asked, rest, preferred_element_type=F32)
        total = sums[pl.ds(0, 512), lanes] + jnp.exp(run_col[:, h : h + 1]) * cross
        mean = jnp.mean(total * total, axis=1, keepdims=True)
        attn_ref[:, lanes] = (
            total * lax.rsqrt(mean + 1e-06) * head_gain_ref[:, lanes]
        ).astype(BF16)

    load_w.wait()
    w_near.wait_recv()
    for made in w_pair:
        made.wait_recv()

    rings_a, rings_b, lasts_a, lasts_b = [], [], [], []
    for s in range(STAGES):
        for which, (rings, axis) in enumerate(((rings_a, "x"), (rings_b, "z"))):
            k = which * STAGES + s
            rings.append(
                RingSum(
                    links,
                    axis,
                    work,
                    k * 4096,
                    1024,
                    1024,
                    work.at[pl.ds(6 * 4096 + k * 1024, 1024)],
                    second.at[pl.ds(k * 2048, 2048)],
                )
            )
        for which, (sums_of, axis) in enumerate(((lasts_a, "z"), (lasts_b, "x"))):
            k = which * STAGES + s
            sums_of.append(
                DirectSum(links, axis, half, k * 1024, 256, last.at[pl.ds(k * 768, 768)])
            )

    def project_quad(s, to):
        quad = s * 4 + to
        k = quad // 3
        chip = (y + k + k // 2 - 2 * (k // 3)) % 4
        w = wide[chip, pl.ds(0, 512), columns(quad % 3 * 512, 512)]
        r = jnp.dot(attn_ref[...], w, preferred_element_type=F32).astype(BF16)
        for u in range(4):
            for side in range(2):
                start = s * 4096 + to * 1024 + (side * 4 + u) * 128
                work[rows_at(start, 128), :] = r[
                    side * 128 : side * 128 + 128, u * UNIT : u * UNIT + UNIT
                ]
                start = (STAGES + s) * 4096 + u * 1024 + (side * 4 + to) * 128
                work[rows_at(start, 128), :] = r[
                    256 + side * 128 : 256 + side * 128 + 128, u * UNIT : u * UNIT + UNIT
                ]

    def project(s):
        def one(i, carry):
            project_quad(s, (x + 3 + i) % 4)
            return carry

        links.group = "sum"
        project_quad(s, (x + 2) % 4)
        rings_a[s].opposite()
        lax.fori_loop(0, 3, one, 0)
        rings_b[s].opposite()
        rings_a[s].direct_up()
        rings_a[s].direct_down()
        rings_b[s].direct_up()
        rings_b[s].direct_down()

    def relay(s):
        links.group = "sum"
        rings_a[s].relay()
        rings_b[s].relay()

    def turn(s):
        links.group = "sum"
        for ring, last_of in ((rings_a[s], lasts_a[s]), (rings_b[s], lasts_b[s])):
            ring.arrived()

            def one(u, carry, ring=ring, last_of=last_of):
                for side in range(2):
                    rows = rows_at(last_of.base + u * 256 + side * 128, 128)
                    half[rows, :] = ring.total(side * 512 + u * 128, 128).astype(BF16)
                return carry

            lax.fori_loop(0, 4, one, 0)
            last_of.send()

    row_moves = [[] for _ in range(STAGES)]
    block = EXPERTS * CAP

    def dispatch(s):
        cols = pl.ds(s * UNIT, UNIT)
        if s == 0:
            for made in resid_moves:
                made.wait_recv()
        links.group = "rows"
        for start, last_of in ((0, lasts_a[s]), (256, lasts_b[s])):
            total = last_of.total() + resid_cols[pl.ds(start, 256), cols].astype(F32)
            hidden[pl.ds(s * 512 + start, 256), :] = total.astype(BF16)
        found = jnp.dot(table[...], hidden[pl.ds(s * 512, 512), :], preferred_element_type=F32)
        pieces[pl.ds(s * block, block), :] = found.astype(BF16)
        lands = rows_in.at[rows_at((s * EXPERTS + me) * CAP, CAP)]
        for step in range(1, EXPERTS):
            to = (me + step) % EXPERTS
            piece = pieces.at[rows_at((s * EXPERTS + to) * CAP, CAP)]
            row_moves[s].append(links.copy(piece, lands, exp_peer(step)))
        lands[...] = pieces[rows_at((s * EXPERTS + me) * CAP, CAP), :]

    squares = [jnp.zeros((CAP, 1), F32)]
    mine = rows_at(ctx * CAP, CAP)
    gathers = [None] * STAGES

    def spread(s, block, side, device):
        cols = pl.ds(s * 2048 + side * 1024, 1024)
        if side == 2:
            cols = pl.ds(s * 2048, 2048)
        ref = tokens.at[rows_at(block * CAP, CAP), cols]
        return links.copy(ref, ref, device)

    def gather(s):
        for made in row_moves[s]:
            made.wait_recv()
        links.group = "gather"
        for u in range(EXPERTS):
            cols = pl.ds((s * EXPERTS + u) * UNIT, UNIT)
            part = rows_in[pl.ds((s * EXPERTS + u) * CAP, CAP), :].astype(F32)
            squares[0] = squares[0] + jnp.sum(part * part, axis=1, keepdims=True)
            tokens[mine, cols] = (part * gain_ref[:, unit_cols(s * EXPERTS + u)]).astype(BF16)
        gathers[s] = dict(
            up_low=spread(s, ctx, 0, along("y", 1)),
            down_high=spread(s, ctx, 1, along("y", -1)),
            up_high=spread(s, ctx, 1, along("y", 1)),
            down_low=spread(s, ctx, 0, along("y", -1)),
            pair=[spread(s, ctx, 2, other_core())],
        )

    from_below, from_above, from_far = below * 2 + core, above * 2 + core, far * 2 + core

    def gather_mid(s):
        links.group = "gather"
        g = gathers[s]
        g["up_low"].wait_recv()
        g["on_up"] = spread(s, from_below, 0, along("y", 1))
        g["near"] = [spread(s, from_below, 0, other_core())]
        g["down_high"].wait_recv()
        g["on_down"] = spread(s, from_above, 1, along("y", -1))
        g["near"].append(spread(s, from_above, 1, other_core()))

    def gather_near(s):
        links.group = "gather"
        g = gathers[s]
        g["up_high"].wait_recv()
        g["near"].append(spread(s, from_below, 1, other_core()))
        g["down_low"].wait_recv()
        g["near"].append(spread(s, from_above, 0, other_core()))

    def gather_far(s):
        links.group = "gather"
        g = gathers[s]
        g["on_up"].wait_recv()
        g["far"] = [spread(s, from_far, 0, other_core())]
        g["on_down"].wait_recv()
        g["far"].append(spread(s, from_far, 1, other_core()))

    def held(s, names):
        for name in names:
            for made in gathers[s][name]:
                made.wait_recv()

    def gate_and_up(s, chip):
        rows = rows_at(chip * (2 * CAP), 2 * CAP)
        total = None
        quad = s * 4
        while quad < s * 4 + 4:
            run = min(3 - quad % 3, s * 4 + 4 - quad)
            start = columns(chip_at(chip, quad // 3) * 1536 + quad % 3 * 512, run * 512)
            part = lax.dot_general(
                tokens[rows, pl.ds(quad * 512, run * 512)],
                gate_up[:, start],
                turned,
                preferred_element_type=F32,
            )
            total = part if total is None else total + part
            quad += run
        if s > 0:
            total = total + sums[rows, :]
        if s < STAGES - 1:
            sums[rows, :] = total
            return
        total = total * scales[rows, 0:1]
        gate, upper = total[:, :576], total[:, 576:]
        active[...] = (gate / (1.0 + jnp.exp(-gate)) * upper).astype(BF16)

    project(0)
    relay(0)
    links.group = "w"
    w_second.wait_recv()
    w_next = spread_w(one_chip, w_all, other_core())
    w_far.append(spread_w(one_chip, w_high, along("y", other_way)))
    w_next.wait_recv()
    project(1)
    turn(0)
    links.group = "w"
    w_far_near = []
    for made, rows in zip(w_far, (w_low, w_high)):
        made.wait_recv()
        w_far_near.append(spread_w(far, rows, other_core()))
    relay(1)
    dispatch(0)
    turn(1)
    for made in w_far_near:
        made.wait_recv()
    project(2)
    gather(0)
    dispatch(1)
    relay(2)
    gather_mid(0)
    gather(1)
    turn(2)
    gather_near(0)
    gather_far(0)
    gather_mid(1)
    dispatch(2)
    links.drain("w")
    load_down = []
    for k in range(4):
        made = pltpu.make_async_copy(
            down_ref.at[:, pl.ds(k * 1536, 1536)], wide.at[k], local.at[3 + k]
        )
        made.start()
        load_down.append(made)
    load_gate.wait()
    load_up.wait()
    held(0, ("pair", "near", "far"))
    gate_and_up(0, y)
    gate_and_up(0, above)
    gather_near(1)
    gate_and_up(0, below)
    gather_far(1)
    gather(2)

    def spread_scale(block, device):
        ref = scales.at[rows_at(block * CAP, CAP)]
        return links.copy(ref, ref, device)

    scale = lax.rsqrt(squares[0] / 6144.0 + 1e-05)
    scales[mine, :] = jnp.broadcast_to(scale, (CAP, UNIT))
    scale_up = spread_scale(ctx, along("y", 1))
    scale_down = spread_scale(ctx, along("y", -1))
    scale_own = spread_scale(ctx, other_core())
    def owned(owner, chip, s):
        return work.at[rows_at(((owner * 4 + chip) * STAGES + s) * block, block)]

    def down(chip):
        moves = []
        for s in range(STAGES):

            def one(quad, carry):
                k = quad // 3
                part = (chip + k + k // 2 - 2 * (k // 3)) % 4
                w = wide[part, :, columns(quad % 3 * 512, 512)]
                o = jnp.dot(active[...], w, preferred_element_type=F32).astype(BF16)
                for owner in range(2):
                    for u in range(4):
                        start = (owner * 4 + chip) * (STAGES * block) + (quad * 4 + u) * CAP
                        work[rows_at(start, CAP), :] = o[
                            owner * CAP : owner * CAP + CAP, u * UNIT : u * UNIT + UNIT
                        ]
                return carry

            lax.fori_loop(4 * s, 4 * s + 4, one, 0)
            lands = partner.at[rows_at((chip * STAGES + s) * block, block)]
            moves.append(links.copy(owned(1 - core, chip, s), lands, other_core()))
        return moves

    def join(chip, moves, s):
        moves[s].wait_recv()
        add_into(owned(core, chip, s), partner.at[rows_at((chip * STAGES + s) * block, block)])

    rings_y = [
        RingSum(
            links,
            "y",
            work,
            core * (4 * STAGES * block) + s * block,
            block,
            STAGES * block,
            first_y.at[pl.ds(s * block, block)],
            second_y.at[pl.ds(s * 2 * block, 2 * block)],
        )
        for s in range(STAGES)
    ]
    held(1, ("pair", "near", "far"))
    gate_and_up(1, y)
    held(2, ("pair",))
    scale_own.wait_recv()
    gate_and_up(2, y)
    gather_mid(2)
    scale_up.wait_recv()
    scale_on = spread_scale(from_below, along("y", 1))
    scale_pair = [spread_scale(from_below, other_core())]
    scale_down.wait_recv()
    scale_pair.append(spread_scale(from_above, other_core()))
    links.drain("sum")
    for made in load_down:
        made.wait()
    links.group = "rest"
    sum_own = down(y)
    gather_near(2)
    scale_on.wait_recv()
    scale_far = spread_scale(from_far, other_core())
    gate_and_up(0, far)
    gate_and_up(1, far)
    gather_far(2)
    links.group = "rest"
    gate_and_up(1, above)
    held(2, ("far",))
    scale_far.wait_recv()
    gate_and_up(2, far)
    sum_far = down(far)
    for s in range(STAGES):
        join(far, sum_far, s)
        rings_y[s].opposite()
    held(2, ("near",))
    for made in scale_pair:
        made.wait_recv()
    gate_and_up(2, above)
    sum_above = down(above)
    gate_and_up(1, below)
    gate_and_up(2, below)
    for s in range(STAGES):
        join(above, sum_above, s)
        rings_y[s].direct_up()
    sum_below = down(below)
    for s in range(STAGES):
        join(below, sum_below, s)
        rings_y[s].direct_down()
    for s in range(STAGES):
        join(y, sum_own, s)

    my_ids = lax.dot_general(
        table[rows_at(me * CAP, CAP), :],
        ids_ref[...].astype(F32).astype(BF16),
        turned,
        preferred_element_type=F32,
    )
    logits = jnp.zeros((CAP, EXPERTS), F32)
    for k in range(4):
        part = routes[:, columns(chip_at(y, k) * 1536, 1536)]
        router_high = part.astype(BF16)
        router_low = (part - router_high.astype(F32)).astype(BF16)
        token = tokens[mine, pl.ds(k * 1536, 1536)]
        for w in (router_high, router_low):
            logits = logits + lax.dot_general(token, w, turned, preferred_element_type=F32)
    gates = 1.0 / (1.0 + jnp.exp(-logits * scale))
    lanes = lax.broadcasted_iota(jnp.int32, (CAP, EXPERTS), 1)
    lanes_f = lanes.astype(F32)
    both = (my_ids[:, 0:1] == lanes_f) | (my_ids[:, 1:2] == lanes_f)
    total = jnp.sum(jnp.where(both, gates, 0.0), axis=1, keepdims=True)
    share = jnp.sum(jnp.where(lanes == me, gates, 0.0), axis=1, keepdims=True) / total
    share = jnp.broadcast_to(share, (CAP, UNIT))

    links.drain("rows")

    back_moves = [[] for _ in range(STAGES)]
    out_moves = []

    def give_back(s):
        rings_y[s].arrived()

        def one(g, carry):
            total = rings_y[s].total(g * CAP, CAP).astype(BF16).astype(F32)
            pieces[rows_at((s * EXPERTS + g) * CAP, CAP), :] = (total * share).astype(BF16)
            return carry

        lax.fori_loop(0, EXPERTS, one, 0)
        lands = back.at[rows_at((s * EXPERTS + me) * CAP, CAP)]
        for step in range(1, EXPERTS):
            to = (me + step) % EXPERTS
            piece = pieces.at[rows_at((s * EXPERTS + to) * CAP, CAP)]
            back_moves[s].append(links.copy(piece, lands, exp_peer(step)))
        lands[...] = pieces[rows_at((s * EXPERTS + me) * CAP, CAP), :]

    def combine(s):
        for made in back_moves[s]:
            made.wait_recv()
        summed = lax.dot_general(
            table[...], back[pl.ds(s * block, block), :], first, preferred_element_type=F32
        )
        rows = pl.ds(s * 512, 512)
        hidden[rows, :] = (hidden[rows, :].astype(F32) + summed).astype(BF16)
        for step in range(1, EXPERTS):
            to = (me + step) % EXPERTS
            part = hidden.at[rows_at(s * 512 + to * 32, 32)]
            out_moves.append(links.copy(part, rows_out.at[s, me], exp_peer(step)))
        rows_out[s, me] = hidden[rows_at(s * 512 + me * 32, 32), :]

    rings_y[0].relay()
    rings_y[1].relay()
    rings_y[2].relay()
    give_back(0)
    give_back(1)
    combine(0)
    give_back(2)
    combine(1)
    combine(2)
    for made in out_moves:
        made.wait_recv()

    def put(g, carry):
        for s in range(STAGES):
            out_ref[:, unit_cols(s * EXPERTS + g)] = rows_out[s, g]
        return carry

    lax.fori_loop(0, EXPERTS, put, 0)
    links.drain("gather")
    links.drain("rest")

    state_pair().wait_send()

    for step in range(1, 4):

        @pl.when((core == 0) & (y + step < 4))
        def _(step=step):
            state_up(step).wait_send()

        @pl.when((core == 0) & (y >= step))
        def _(step=step):
            state_over(step).wait_send()


def layer(*arrays):
    vmem = pl.BlockSpec(memory_space=pltpu.VMEM)
    hbm = pl.BlockSpec(memory_space=pl.ANY)

    def rows(n, width=UNIT):
        return pltpu.VMEM((n, width), BF16)

    block = EXPERTS * CAP
    return pl.pallas_call(
        layer_kernel,
        out_shape=jax.ShapeDtypeStruct((32, 6144), BF16),
        in_specs=[hbm] * 3 + [vmem] * 2 + [hbm] * 2 + [vmem] * 2 + [hbm] * 4,
        out_specs=vmem,
        scratch_shapes=[
            rows(512, 512),
            rows(512, 512),
            rows(512, 512),
            rows(32, 6144),
            pltpu.VMEM((EXPERTS, 6144), F32),
            rows(528),
            rows(528),
            pltpu.VMEM((4, 528, 128), BF16),
            pltpu.VMEM((512, 128), F32),
            pltpu.VMEM((4, 128), F32),
            rows(512, 512),
            pltpu.VMEM((4, 576, 1536), BF16),
            rows(1152, 6144),
            rows(24 * block),
            rows(6 * 2048),
            rows(6 * 1024),
            rows(6 * 768),
            pltpu.VMEM((EXPERTS, 32, STAGES * UNIT), BF16),
            rows(512, STAGES * UNIT),
            rows(STAGES * 512),
            rows(block, 512),
            rows(STAGES * block),
            rows(STAGES * block),
            rows(8 * CAP, 6144),
            pltpu.VMEM((8 * CAP, UNIT), F32),
            pltpu.VMEM((8 * CAP, 1152), F32),
            rows(2 * CAP, 576),
            rows(4 * STAGES * block),
            rows(STAGES * block),
            rows(2 * STAGES * block),
            rows(STAGES * block),
            pltpu.VMEM((STAGES, EXPERTS, 32, UNIT), BF16),
            pltpu.SemaphoreType.DMA((12,)),
            pltpu.SemaphoreType.DMA((LINKS,)),
            pltpu.SemaphoreType.DMA((LINKS,)),
            pltpu.SemaphoreType.DMA((8,)),
            pltpu.SemaphoreType.DMA((8,)),
        ],
        compiler_params=pltpu.CompilerParams(
            collective_id=0, has_side_effects=True, vmem_limit_bytes=65000 << 10
        ),
        name="layer",
    )(*arrays)


def per_device(
    query_rows,
    key_rows,
    value_rows,
    log_decay,
    attn_gain,
    out_weight,
    residual,
    ffn_gain,
    router,
    expert_ids,
    w_gate,
    w_up,
    w_down,
):
    return layer(
        query_rows,
        key_rows,
        value_rows,
        log_decay.T,
        attn_gain.reshape(1, -1),
        out_weight,
        residual,
        expert_ids.T,
        ffn_gain.reshape(1, -1),
        router.T,
        w_gate[0].T,
        w_up[0].T,
        w_down[0],
    )


def solution(mesh):
    return jax.shard_map(
        per_device,
        mesh=mesh,
        in_specs=(
            P("ctx", "exp"),
            P("ctx", "exp"),
            P("ctx", "exp"),
            P("ctx", "exp"),
            P("exp"),
            P("exp", "ctx"),
            P(("ctx", "exp"), None),
            P(),
            P(),
            P("ctx", None),
            P("exp", None, "ctx"),
            P("exp", None, "ctx"),
            P("exp", "ctx", None),
        ),
        out_specs=P(("ctx", "exp"), None),
        check_vma=False,
    )
```

```python
import functools

import jax
import jax.numpy as jnp
from jax import lax
from jax.experimental import pallas as pl
from jax.experimental.pallas import tpu as pltpu
from jax.sharding import PartitionSpec as P

MESH = pl.DeviceIdType.MESH
F32 = jnp.float32
BF16 = jnp.bfloat16
EXPERTS = 16
CAP = 80
UNIT = 128
STAGES = 3
LINKS = 304


def place():
    ctx = lax.axis_index("ctx")
    exp = lax.axis_index("exp")
    return ctx // 2, ctx % 2, exp // 4, exp % 4


def along(axis, step):
    y, core, x, z = place()
    step = step % 4
    if axis == "x":
        return (y * 2 + core, (x + step) % 4 * 4 + z)
    if axis == "z":
        return (y * 2 + core, x * 4 + (z + step) % 4)
    return ((y + step) % 4 * 2 + core, x * 4 + z)


def exp_peer(step):
    return (lax.axis_index("ctx"), (lax.axis_index("exp") + step) % EXPERTS)


def ctx_peer(step):
    return ((lax.axis_index("ctx") + step) % 8, lax.axis_index("exp"))


def other_core():
    y, core, _, _ = place()
    return (y * 2 + 1 - core, lax.axis_index("exp"))


class Links:
    def __init__(self, send, recv):
        self.send, self.recv, self.count = send, recv, 0
        self.open, self.group, self.early = {}, "w", None

    def copy(self, src, dst, device):
        made = pltpu.make_async_remote_copy(
            src_ref=src,
            dst_ref=dst,
            send_sem=self.send.at[self.count],
            recv_sem=self.recv.at[self.count],
            device_id=device,
            device_id_type=MESH,
        )
        made.start()
        self.count += 1
        assert self.count <= LINKS
        self.open.setdefault(self.group, []).append(made)
        return made

    def drain(self, group):
        for made in self.open.pop(group, []):
            if made is not self.early:
                made.wait_send()


def add_into(target, extra):
    size = 128 if target.shape[0] % 128 == 0 else 80

    def one(i, carry):
        rows = rows_at(i * size, size)
        target[rows, :] = (target[rows, :].astype(F32) + extra[rows, :].astype(F32)).astype(BF16)
        return carry

    lax.fori_loop(0, target.shape[0] // size, one, 0)


class RingSum:
    def __init__(self, links, axis, part, base, n, stride, first, second):
        place_of = dict(zip(("y", "core", "x", "z"), place()))
        self.links, self.axis, self.i = links, axis, place_of[axis]
        self.part, self.base, self.n, self.stride = part, base, n, stride
        self.first, self.second = first, second

    def low(self, d):
        return self.part.at[rows_at(self.base + d * self.stride, self.n // 2)]

    def high(self, d):
        return self.part.at[rows_at(self.base + d * self.stride + self.n // 2, self.n // 2)]

    def slot(self, k):
        return pl.ds(k * (self.n // 2), self.n // 2)

    def opposite(self):
        far, slot = (self.i + 2) % 4, self.slot
        up = self.links.copy(self.low(far), self.first.at[slot(0)], along(self.axis, 1))
        down = self.links.copy(self.high(far), self.first.at[slot(1)], along(self.axis, -1))
        self.far = (up, down)

    def direct_up(self):
        up, slot = (self.i + 1) % 4, self.slot
        self.near = [self.links.copy(self.high(up), self.second.at[slot(1)], along(self.axis, 1))]

    def direct_down(self):
        down, slot = (self.i + 3) % 4, self.slot
        self.near.append(
            self.links.copy(self.low(down), self.second.at[slot(2)], along(self.axis, -1))
        )

    def relay(self):
        up, down, slot = (self.i + 1) % 4, (self.i + 3) % 4, self.slot
        self.far[0].wait_recv()
        add_into(self.low(up), self.first.at[slot(0)])
        self.near.append(
            self.links.copy(self.low(up), self.second.at[slot(0)], along(self.axis, 1))
        )
        self.far[1].wait_recv()
        add_into(self.high(down), self.first.at[slot(1)])
        self.near.append(
            self.links.copy(self.high(down), self.second.at[slot(3)], along(self.axis, -1))
        )

    def arrived(self):
        for made in self.near:
            made.wait_recv()

    def total(self, start, size):
        own = self.part[rows_at(self.base + self.i * self.stride + start, size), :].astype(F32)
        own = own + self.second[rows_at(start, size), :].astype(F32)
        return own + self.second[rows_at(self.n + start, size), :].astype(F32)


class DirectSum:
    def __init__(self, links, axis, part, base, n, landed):
        place_of = dict(zip(("y", "core", "x", "z"), place()))
        self.links, self.axis, self.i = links, axis, place_of[axis]
        self.part, self.base, self.n, self.landed = part, base, n, landed

    def send(self):
        self.moves = [
            self.links.copy(
                self.part.at[rows_at(self.base + (self.i + step) % 4 * self.n, self.n)],
                self.landed.at[pl.ds((step - 1) * self.n, self.n)],
                along(self.axis, step),
            )
            for step in (2, 1, 3)
        ]

    def total(self):
        for made in self.moves:
            made.wait_recv()
        total = self.part[rows_at(self.base + self.i * self.n, self.n), :].astype(F32)
        for k in range(3):
            total = total + self.landed[pl.ds(k * self.n, self.n), :].astype(F32)
        return total


def columns(start, size):
    return pl.ds(pl.multiple_of(start, 128), size)


def rows_at(start, size):
    return pl.ds(pl.multiple_of(start, 16), size)


def split3(value):
    one = value.astype(BF16)
    rest = value - one.astype(F32)
    two = rest.astype(BF16)
    return one, two, (rest - two.astype(F32)).astype(BF16)


def layer_kernel(
    query_ref,
    key_ref,
    value_ref,
    decay_ref,
    head_gain_ref,
    out_w_ref,
    resid_ref,
    ids_ref,
    gain_ref,
    router_ref,
    gate_ref,
    up_ref,
    down_ref,
    out_ref,
    query,
    key,
    value,
    resid,
    routes,
    state,
    chip_state,
    states,
    carried,
    gone,
    attn_ref,
    wide,
    gate_up,
    work,
    second,
    half,
    last,
    resid_parts,
    resid_cols,
    hidden,
    table,
    pieces,
    rows_in,
    tokens,
    scales,
    sums,
    active,
    partner,
    first_y,
    second_y,
    back,
    rows_out,
    local,
    send,
    recv,
    state_send,
    state_recv,
):
    y, core, x, z = place()
    ctx = y * 2 + core
    me = lax.axis_index("exp")
    links = Links(send, recv)
    above, below, far = (y + 1) % 4, (y + 3) % 4, (y + 2) % 4

    def chip_at(home, k):
        return (home + (0, 1, 3, 2)[k]) % 4

    def unit_cols(j):
        k = j // 12
        chip = (y + k + k // 2 - 2 * (k // 3)) % 4
        return columns(chip * 1536 + j % 12 * UNIT, UNIT)

    barrier = pltpu.get_barrier_semaphore()
    for device in [along("y", 1), along("y", 3), other_core(), along("y", 2)]:
        pl.semaphore_signal(barrier, inc=1, device_id=device, device_id_type=MESH)
    for step in range(1, EXPERTS):
        pl.semaphore_signal(barrier, inc=1, device_id=exp_peer(step), device_id_type=MESH)

    load_gate = pltpu.make_async_copy(gate_ref, gate_up.at[pl.ds(0, 576)], local.at[1])
    load_up = pltpu.make_async_copy(up_ref, gate_up.at[pl.ds(576, 576)], local.at[2])
    w_all, w_low, w_high = pl.ds(0, 512), pl.ds(0, 256), pl.ds(256, 256)
    one_way, other_way = (2 * core + 3) % 4, (2 * core + 1) % 4
    one_chip, other_chip = (y + one_way) % 4, (y + other_way) % 4

    def w_part(chip, side, rows):
        return wide.at[chip, rows, columns(side * 768, 768)]

    load_in = []
    for k, (src, dst) in enumerate(
        (
            (key_ref, key),
            (value_ref, value),
            (query_ref, query),
            (resid_ref, resid),
            (router_ref, routes),
        )
    ):
        made = pltpu.make_async_copy(src, dst, local.at[7 + k])
        made.start()
        load_in.append(made)
    load_w = pltpu.make_async_copy(out_w_ref, w_part(y, core, w_all), local.at[0])
    load_w.start()

    earlier = lax.broadcasted_iota(jnp.int32, (512, 512), 1) <= lax.broadcasted_iota(
        jnp.int32, (512, 512), 0
    )
    lower = jnp.where(earlier, 1.0, 0.0).astype(BF16)
    turned = (((1,), (1,)), ((), ()))
    first = (((0,), (0,)), ((), ()))
    run_col = jnp.zeros((512, 4), F32)
    run_row = jnp.zeros((4, 512), F32)
    for term in split3(decay_ref[...]):
        run_col = run_col + lax.dot_general(lower, term, turned, preferred_element_type=F32)
        run_row = run_row + lax.dot_general(term, lower, turned, preferred_element_type=F32)
    load_in[0].wait()
    load_in[1].wait()
    lines = lax.broadcasted_iota(jnp.int32, (4, 128), 0)
    ends = jnp.zeros((4, 128), F32)
    for h in range(4):
        lanes = pl.ds(h * 128, 128)
        end = run_col[511:512, h : h + 1]
        to_end = jnp.exp(end - run_col[:, h : h + 1])
        decayed = (key[:, lanes].astype(F32) * to_end).astype(BF16)
        own = lax.dot_general(decayed, value[:, lanes], first, preferred_element_type=F32)
        state[pl.ds(h * 128, 128), :] = own.astype(BF16)
        ends = jnp.where(lines == h, end, ends)

    def pack_ends(value):
        parts = [t.astype(F32) for t in split3(value)]
        return jnp.concatenate(parts + [jnp.zeros((4, 128), F32)], axis=0).astype(BF16)

    def ends_of(ref):
        value = ref[pl.ds(512, 16), :].astype(F32)
        return value[0:4] + value[4:8] + value[8:12]

    state[pl.ds(512, 16), :] = pack_ends(ends)

    pl.semaphore_wait(barrier, EXPERTS + 3)

    def state_copy(src, dst, k, device):
        return pltpu.make_async_remote_copy(
            src_ref=src,
            dst_ref=dst,
            send_sem=state_send.at[k],
            recv_sem=state_recv.at[k],
            device_id=device,
            device_id_type=MESH,
        )

    def state_pair():
        return state_copy(state, states.at[0], 0, other_core())

    def state_up(step):
        return state_copy(chip_state, states.at[step], step, along("y", step))

    def state_over(step):
        return state_copy(states.at[step], states.at[step], 4 + step, other_core())

    state_pair().start()

    def spread_w(chip, rows, device):
        src = out_w_ref if chip is None else w_part(chip, core, rows)
        return links.copy(src, w_part(y if chip is None else chip, core, rows), device)

    w_first = spread_w(None, w_all, along("y", one_way))
    w_pair = [spread_w(None, w_all, other_core())]

    state_pair().wait_recv()

    @pl.when(core == 0)
    def _():
        pair_ends = ends_of(states.at[0])
        for h in range(4):
            rows = pl.ds(h * 128, 128)
            joined = jnp.exp(pair_ends[h : h + 1]) * state[rows, :].astype(F32)
            chip_state[rows, :] = (joined + states[0, rows, :].astype(F32)).astype(BF16)
        chip_state[pl.ds(512, 16), :] = pack_ends(pair_ends + ends_of(state))
        for step in range(1, 4):

            @pl.when(y + step < 4)
            def _(step=step):
                state_up(step).start()

    load_gate.start()
    load_up.start()

    for made in load_in[2:]:
        made.wait()

    def resid_part(g, carry):
        for s in range(STAGES):
            resid_parts[g, :, pl.ds(s * UNIT, UNIT)] = resid[:, unit_cols(s * EXPERTS + g)]
        return carry

    lax.fori_loop(0, EXPERTS, resid_part, 0)
    resid_moves = []
    links.group = "rows"
    for step in range(1, EXPERTS):
        to = (me + step) % EXPERTS
        resid_moves.append(
            links.copy(resid_parts.at[to], resid_cols.at[rows_at(me * 32, 32)], exp_peer(step))
        )
    resid_cols[rows_at(me * 32, 32), :] = resid_parts[me]

    for h in range(4):
        lanes = pl.ds(h * 128, 128)
        for r in range(2):
            seen = (r + 1) * 256
            rows = pl.ds(r * 256, 256)
            scores = lax.dot_general(
                query[rows, lanes],
                key[pl.ds(0, seen), lanes],
                turned,
                preferred_element_type=F32,
            )
            spread_of = run_col[r * 256 : seen, h : h + 1] - run_row[h : h + 1, :seen]
            late = lax.broadcasted_iota(jnp.int32, (256, seen), 0) + r * 256
            soon = lax.broadcasted_iota(jnp.int32, (256, seen), 1)
            decay = jnp.where(late >= soon, jnp.exp(jnp.minimum(spread_of, 0.0)), 0.0)
            sums[rows, lanes] = jnp.dot(
                (scores * decay).astype(BF16),
                value[pl.ds(0, seen), lanes],
                preferred_element_type=F32,
            )

    for step in range(1, 4):

        @pl.when((core == 0) & (y >= step))
        def _(step=step):
            state_up(step).wait_recv()
            state_over(step).start()

    links.group = "w"
    w_first.wait_send()
    links.early = w_first
    w_second = spread_w(None, w_all, along("y", other_way))
    w_first.wait_recv()
    w_near = spread_w(other_chip, w_all, other_core())
    w_far = [spread_w(other_chip, w_low, along("y", one_way))]

    experts = lax.broadcasted_iota(jnp.int32, (EXPERTS, 512), 0)
    picked = (ids_ref[0:1, :] == experts) | (ids_ref[1:2, :] == experts)
    before = lax.broadcasted_iota(jnp.int32, (512, 512), 0) < lax.broadcasted_iota(
        jnp.int32, (512, 512), 1
    )
    rank = jnp.dot(
        jnp.where(picked, 1.0, 0.0).astype(BF16),
        jnp.where(before, 1.0, 0.0).astype(BF16),
        preferred_element_type=F32,
    )
    code = jnp.where(picked, rank, -1.0)
    slots = lax.broadcasted_iota(jnp.int32, (CAP, 512), 0).astype(F32)
    for e in range(EXPERTS):
        table[pl.ds(e * CAP, CAP), :] = jnp.where(code[e : e + 1, :] == slots, 1.0, 0.0).astype(
            BF16
        )

    carried[...] = jnp.zeros((512, 128), F32)
    gone[...] = jnp.zeros((4, 128), F32)
    for step in range(1, 4):

        @pl.when((core == 1) & (y >= step))
        def _(step=step):
            state_over(step).wait_recv()

        @pl.when(y >= step)
        def _(step=step):
            for h in range(4):
                rows = pl.ds(h * 128, 128)
                kept = jnp.exp(gone[pl.ds(h, 1), :])
                carried[rows, :] = carried[rows, :] + kept * states[step, rows, :].astype(F32)
            gone[...] = gone[...] + ends_of(states.at[step])

    @pl.when(core == 1)
    def _():
        pair_ends = ends_of(states.at[0])
        for h in range(4):
            rows = pl.ds(h * 128, 128)
            kept = jnp.exp(pair_ends[h : h + 1])
            carried[rows, :] = kept * carried[rows, :] + states[0, rows, :].astype(F32)

    for h in range(4):
        lanes = pl.ds(h * 128, 128)
        full = carried[lanes, :]
        near = full.astype(BF16)
        rest = (full - near.astype(F32)).astype(BF16)
        asked = query[:, lanes]
        cross = jnp.dot(asked, near, preferred_element_type=F32)
        cross = cross + jnp.dot(asked, rest, preferred_element_type=F32)
        total = sums[pl.ds(0, 512), lanes] + jnp.exp(run_col[:, h : h + 1]) * cross
        mean = jnp.mean(total * total, axis=1, keepdims=True)
        attn_ref[:, lanes] = (
            total * lax.rsqrt(mean + 1e-06) * head_gain_ref[:, lanes]
        ).astype(BF16)

    load_w.wait()
    w_near.wait_recv()
    for made in w_pair:
        made.wait_recv()

    rings_a, rings_b, lasts_a, lasts_b = [], [], [], []
    for s in range(STAGES):
        for which, (rings, axis) in enumerate(((rings_a, "x"), (rings_b, "z"))):
            k = which * STAGES + s
            rings.append(
                RingSum(
                    links,
                    axis,
                    work,
                    k * 4096,
                    1024,
                    1024,
                    work.at[pl.ds(6 * 4096 + k * 1024, 1024)],
                    second.at[pl.ds(k * 2048, 2048)],
                )
            )
        for which, (sums_of, axis) in enumerate(((lasts_a, "z"), (lasts_b, "x"))):
            k = which * STAGES + s
            sums_of.append(
                DirectSum(links, axis, half, k * 1024, 256, last.at[pl.ds(k * 768, 768)])
            )

    def project_quad(s, to):
        quad = s * 4 + to
        k = quad // 3
        chip = (y + k + k // 2 - 2 * (k // 3)) % 4
        w = wide[chip, pl.ds(0, 512), columns(quad % 3 * 512, 512)]
        r = jnp.dot(attn_ref[...], w, preferred_element_type=F32).astype(BF16)
        for u in range(4):
            for side in range(2):
                start = s * 4096 + to * 1024 + (side * 4 + u) * 128
                work[rows_at(start, 128), :] = r[
                    side * 128 : side * 128 + 128, u * UNIT : u * UNIT + UNIT
                ]
                start = (STAGES + s) * 4096 + u * 1024 + (side * 4 + to) * 128
                work[rows_at(start, 128), :] = r[
                    256 + side * 128 : 256 + side * 128 + 128, u * UNIT : u * UNIT + UNIT
                ]

    def project(s):
        def one(i, carry):
            project_quad(s, (x + 3 + i) % 4)
            return carry

        links.group = "sum"
        project_quad(s, (x + 2) % 4)
        rings_a[s].opposite()
        lax.fori_loop(0, 3, one, 0)
        rings_b[s].opposite()
        rings_a[s].direct_up()
        rings_a[s].direct_down()
        rings_b[s].direct_up()
        rings_b[s].direct_down()

    def relay(s):
        links.group = "sum"
        rings_a[s].relay()
        rings_b[s].relay()

    def turn(s):
        links.group = "sum"
        for ring, last_of in ((rings_a[s], lasts_a[s]), (rings_b[s], lasts_b[s])):
            ring.arrived()

            def one(u, carry, ring=ring, last_of=last_of):
                for side in range(2):
                    rows = rows_at(last_of.base + u * 256 + side * 128, 128)
                    half[rows, :] = ring.total(side * 512 + u * 128, 128).astype(BF16)
                return carry

            lax.fori_loop(0, 4, one, 0)
            last_of.send()

    row_moves = [[] for _ in range(STAGES)]
    block = EXPERTS * CAP

    def dispatch(s):
        cols = pl.ds(s * UNIT, UNIT)
        if s == 0:
            for made in resid_moves:
                made.wait_recv()
        links.group = "rows"
        for start, last_of in ((0, lasts_a[s]), (256, lasts_b[s])):
            total = last_of.total() + resid_cols[pl.ds(start, 256), cols].astype(F32)
            hidden[pl.ds(s * 512 + start, 256), :] = total.astype(BF16)
        found = jnp.dot(table[...], hidden[pl.ds(s * 512, 512), :], preferred_element_type=F32)
        pieces[pl.ds(s * block, block), :] = found.astype(BF16)
        lands = rows_in.at[rows_at((s * EXPERTS + me) * CAP, CAP)]
        for step in range(1, EXPERTS):
            to = (me + step) % EXPERTS
            piece = pieces.at[rows_at((s * EXPERTS + to) * CAP, CAP)]
            row_moves[s].append(links.copy(piece, lands, exp_peer(step)))
        lands[...] = pieces[rows_at((s * EXPERTS + me) * CAP, CAP), :]

    squares = [jnp.zeros((CAP, 1), F32)]
    mine = rows_at(ctx * CAP, CAP)
    gathers = [None] * STAGES

    def spread(s, block, side, device):
        cols = pl.ds(s * 2048 + side * 1024, 1024)
        if side == 2:
            cols = pl.ds(s * 2048, 2048)
        ref = tokens.at[rows_at(block * CAP, CAP), cols]
        return links.copy(ref, ref, device)

    def gather(s):
        for made in row_moves[s]:
            made.wait_recv()
        links.group = "gather"
        for u in range(EXPERTS):
            cols = pl.ds((s * EXPERTS + u) * UNIT, UNIT)
            part = rows_in[pl.ds((s * EXPERTS + u) * CAP, CAP), :].astype(F32)
            squares[0] = squares[0] + jnp.sum(part * part, axis=1, keepdims=True)
            tokens[mine, cols] = (part * gain_ref[:, unit_cols(s * EXPERTS + u)]).astype(BF16)
        gathers[s] = dict(
            up_low=spread(s, ctx, 0, along("y", 1)),
            down_high=spread(s, ctx, 1, along("y", -1)),
            pair=[spread(s, ctx, 2, other_core())],
        )

    def gather_late(s):
        links.group = "gather"
        gathers[s]["up_high"] = spread(s, ctx, 1, along("y", 1))
        gathers[s]["down_low"] = spread(s, ctx, 0, along("y", -1))

    from_below, from_above, from_far = below * 2 + core, above * 2 + core, far * 2 + core

    def gather_mid(s):
        links.group = "gather"
        g = gathers[s]
        g["up_low"].wait_recv()
        g["on_up"] = spread(s, from_below, 0, along("y", 1))
        g["near"] = [spread(s, from_below, 0, other_core())]
        g["down_high"].wait_recv()
        g["on_down"] = spread(s, from_above, 1, along("y", -1))
        g["near"].append(spread(s, from_above, 1, other_core()))

    def gather_near(s):
        links.group = "gather"
        g = gathers[s]
        g["up_high"].wait_recv()
        g["near"].append(spread(s, from_below, 1, other_core()))
        g["down_low"].wait_recv()
        g["near"].append(spread(s, from_above, 0, other_core()))

    def gather_far(s):
        links.group = "gather"
        g = gathers[s]
        g["on_up"].wait_recv()
        g["far"] = [spread(s, from_far, 0, other_core())]
        g["on_down"].wait_recv()
        g["far"].append(spread(s, from_far, 1, other_core()))

    def held(s, names):
        for name in names:
            for made in gathers[s][name]:
                made.wait_recv()

    def gate_and_up(s, chip):
        rows = rows_at(chip * (2 * CAP), 2 * CAP)
        total = None
        quad = s * 4
        while quad < s * 4 + 4:
            run = min(3 - quad % 3, s * 4 + 4 - quad)
            start = columns(chip_at(chip, quad // 3) * 1536 + quad % 3 * 512, run * 512)
            part = lax.dot_general(
                tokens[rows, pl.ds(quad * 512, run * 512)],
                gate_up[:, start],
                turned,
                preferred_element_type=F32,
            )
            total = part if total is None else total + part
            quad += run
        if s > 0:
            total = total + sums[rows, :]
        if s < STAGES - 1:
            sums[rows, :] = total
            return
        total = total * scales[rows, 0:1]
        gate, upper = total[:, :576], total[:, 576:]
        active[...] = (gate / (1.0 + jnp.exp(-gate)) * upper).astype(BF16)

    project(0)
    relay(0)
    links.group = "w"
    w_second.wait_recv()
    w_next = spread_w(one_chip, w_all, other_core())
    w_far.append(spread_w(one_chip, w_high, along("y", other_way)))
    w_next.wait_recv()
    project(1)
    turn(0)
    links.group = "w"
    w_far_near = []
    for made, rows in zip(w_far, (w_low, w_high)):
        made.wait_recv()
        w_far_near.append(spread_w(far, rows, other_core()))
    relay(1)
    dispatch(0)
    turn(1)
    for made in w_far_near:
        made.wait_recv()
    project(2)
    gather(0)
    dispatch(1)
    gather_late(0)
    relay(2)
    gather_mid(0)
    gather(1)
    turn(2)
    gather_late(1)
    gather_near(0)
    gather_far(0)
    gather_mid(1)
    dispatch(2)
    links.drain("w")
    load_down = []
    for k in range(4):
        made = pltpu.make_async_copy(
            down_ref.at[:, pl.ds(k * 1536, 1536)], wide.at[k], local.at[3 + k]
        )
        made.start()
        load_down.append(made)
    load_gate.wait()
    load_up.wait()
    held(0, ("pair", "near", "far"))
    gate_and_up(0, y)
    gate_and_up(0, above)
    gather_near(1)
    gate_and_up(0, below)
    gather_far(1)
    gather(2)

    def spread_scale(block, device):
        ref = scales.at[rows_at(block * CAP, CAP)]
        return links.copy(ref, ref, device)

    scale = lax.rsqrt(squares[0] / 6144.0 + 1e-05)
    scales[mine, :] = jnp.broadcast_to(scale, (CAP, UNIT))
    scale_up = spread_scale(ctx, along("y", 1))
    scale_down = spread_scale(ctx, along("y", -1))
    scale_own = spread_scale(ctx, other_core())
    def owned(owner, chip, s):
        return work.at[rows_at(((owner * 4 + chip) * STAGES + s) * block, block)]

    def down(chip):
        moves = []
        for s in range(STAGES):

            def one(quad, carry):
                k = quad // 3
                part = (chip + k + k // 2 - 2 * (k // 3)) % 4
                w = wide[part, :, columns(quad % 3 * 512, 512)]
                o = jnp.dot(active[...], w, preferred_element_type=F32).astype(BF16)
                for owner in range(2):
                    for u in range(4):
                        start = (owner * 4 + chip) * (STAGES * block) + (quad * 4 + u) * CAP
                        work[rows_at(start, CAP), :] = o[
                            owner * CAP : owner * CAP + CAP, u * UNIT : u * UNIT + UNIT
                        ]
                return carry

            lax.fori_loop(4 * s, 4 * s + 4, one, 0)
            lands = partner.at[rows_at((chip * STAGES + s) * block, block)]
            moves.append(links.copy(owned(1 - core, chip, s), lands, other_core()))
        return moves

    def join(chip, moves, s):
        moves[s].wait_recv()
        add_into(owned(core, chip, s), partner.at[rows_at((chip * STAGES + s) * block, block)])

    rings_y = [
        RingSum(
            links,
            "y",
            work,
            core * (4 * STAGES * block) + s * block,
            block,
            STAGES * block,
            first_y.at[pl.ds(s * block, block)],
            second_y.at[pl.ds(s * 2 * block, 2 * block)],
        )
        for s in range(STAGES)
    ]
    held(1, ("pair", "near", "far"))
    gate_and_up(1, y)
    held(2, ("pair",))
    scale_own.wait_recv()
    gate_and_up(2, y)
    gather_late(2)
    gather_mid(2)
    scale_up.wait_recv()
    scale_on = spread_scale(from_below, along("y", 1))
    scale_pair = [spread_scale(from_below, other_core())]
    scale_down.wait_recv()
    scale_pair.append(spread_scale(from_above, other_core()))
    links.drain("sum")
    for made in load_down:
        made.wait()
    links.group = "rest"
    sum_own = down(y)
    gather_near(2)
    scale_on.wait_recv()
    scale_far = spread_scale(from_far, other_core())
    gate_and_up(0, far)
    gate_and_up(1, far)
    gather_far(2)
    links.group = "rest"
    gate_and_up(1, above)
    held(2, ("far",))
    scale_far.wait_recv()
    gate_and_up(2, far)
    sum_far = down(far)
    join(far, sum_far, 0)
    rings_y[0].opposite()
    held(2, ("near",))
    for made in scale_pair:
        made.wait_recv()
    gate_and_up(2, above)
    join(far, sum_far, 1)
    rings_y[1].opposite()
    sum_above = down(above)
    join(far, sum_far, 2)
    rings_y[2].opposite()
    gate_and_up(1, below)
    gate_and_up(2, below)
    for s in range(STAGES):
        join(above, sum_above, s)
        if s < 2:
            rings_y[s].direct_up()
    sum_below = down(below)
    join(below, sum_below, 0)
    rings_y[0].direct_down()
    rings_y[0].relay()
    join(below, sum_below, 1)
    rings_y[1].direct_down()
    join(below, sum_below, 2)
    for s in range(STAGES):
        join(y, sum_own, s)

    my_ids = lax.dot_general(
        table[rows_at(me * CAP, CAP), :],
        ids_ref[...].astype(F32).astype(BF16),
        turned,
        preferred_element_type=F32,
    )
    logits = jnp.zeros((CAP, EXPERTS), F32)
    for k in range(4):
        part = routes[:, columns(chip_at(y, k) * 1536, 1536)]
        router_high = part.astype(BF16)
        router_low = (part - router_high.astype(F32)).astype(BF16)
        token = tokens[mine, pl.ds(k * 1536, 1536)]
        for w in (router_high, router_low):
            logits = logits + lax.dot_general(token, w, turned, preferred_element_type=F32)
    gates = 1.0 / (1.0 + jnp.exp(-logits * scale))
    lanes = lax.broadcasted_iota(jnp.int32, (CAP, EXPERTS), 1)
    lanes_f = lanes.astype(F32)
    both = (my_ids[:, 0:1] == lanes_f) | (my_ids[:, 1:2] == lanes_f)
    total = jnp.sum(jnp.where(both, gates, 0.0), axis=1, keepdims=True)
    share = jnp.sum(jnp.where(lanes == me, gates, 0.0), axis=1, keepdims=True) / total
    share = jnp.broadcast_to(share, (CAP, UNIT))

    links.drain("rows")

    back_moves = [[] for _ in range(STAGES)]
    out_moves = []

    def give_back(s):
        rings_y[s].arrived()

        lands = back.at[rows_at((s * EXPERTS + me) * CAP, CAP)]
        for step in list(range(1, EXPERTS)) + [0]:
            to = (me + step) % EXPERTS
            total = rings_y[s].total(to * CAP, CAP).astype(BF16).astype(F32)
            piece = pieces.at[rows_at((s * EXPERTS + to) * CAP, CAP)]
            if step == 0:
                lands[...] = (total * share).astype(BF16)
                continue
            piece[...] = (total * share).astype(BF16)
            back_moves[s].append(links.copy(piece, lands, exp_peer(step)))

    def combine(s):
        for made in back_moves[s]:
            made.wait_recv()
        summed = lax.dot_general(
            table[...], back[pl.ds(s * block, block), :], first, preferred_element_type=F32
        )
        rows = pl.ds(s * 512, 512)
        hidden[rows, :] = (hidden[rows, :].astype(F32) + summed).astype(BF16)
        for step in range(1, EXPERTS):
            to = (me + step) % EXPERTS
            part = hidden.at[rows_at(s * 512 + to * 32, 32)]
            out_moves.append(links.copy(part, rows_out.at[s, me], exp_peer(step)))
        rows_out[s, me] = hidden[rows_at(s * 512 + me * 32, 32), :]

    rings_y[1].relay()
    rings_y[2].direct_up()
    rings_y[2].direct_down()
    give_back(0)
    rings_y[2].relay()
    give_back(1)
    combine(0)
    give_back(2)
    combine(1)
    combine(2)
    for made in out_moves:
        made.wait_recv()

    def put(g, carry):
        for s in range(STAGES):
            out_ref[:, unit_cols(s * EXPERTS + g)] = rows_out[s, g]
        return carry

    lax.fori_loop(0, EXPERTS, put, 0)
    links.drain("gather")
    links.drain("rest")

    state_pair().wait_send()

    for step in range(1, 4):

        @pl.when((core == 0) & (y + step < 4))
        def _(step=step):
            state_up(step).wait_send()

        @pl.when((core == 0) & (y >= step))
        def _(step=step):
            state_over(step).wait_send()


def layer(*arrays):
    vmem = pl.BlockSpec(memory_space=pltpu.VMEM)
    hbm = pl.BlockSpec(memory_space=pl.ANY)

    def rows(n, width=UNIT):
        return pltpu.VMEM((n, width), BF16)

    block = EXPERTS * CAP
    return pl.pallas_call(
        layer_kernel,
        out_shape=jax.ShapeDtypeStruct((32, 6144), BF16),
        in_specs=[hbm] * 3 + [vmem] * 2 + [hbm] * 2 + [vmem] * 2 + [hbm] * 4,
        out_specs=vmem,
        scratch_shapes=[
            rows(512, 512),
            rows(512, 512),
            rows(512, 512),
            rows(32, 6144),
            pltpu.VMEM((EXPERTS, 6144), F32),
            rows(528),
            rows(528),
            pltpu.VMEM((4, 528, 128), BF16),
            pltpu.VMEM((512, 128), F32),
            pltpu.VMEM((4, 128), F32),
            rows(512, 512),
            pltpu.VMEM((4, 576, 1536), BF16),
            rows(1152, 6144),
            rows(24 * block),
            rows(6 * 2048),
            rows(6 * 1024),
            rows(6 * 768),
            pltpu.VMEM((EXPERTS, 32, STAGES * UNIT), BF16),
            rows(512, STAGES * UNIT),
            rows(STAGES * 512),
            rows(block, 512),
            rows(STAGES * block),
            rows(STAGES * block),
            rows(8 * CAP, 6144),
            pltpu.VMEM((8 * CAP, UNIT), F32),
            pltpu.VMEM((8 * CAP, 1152), F32),
            rows(2 * CAP, 576),
            rows(4 * STAGES * block),
            rows(STAGES * block),
            rows(2 * STAGES * block),
            rows(STAGES * block),
            pltpu.VMEM((STAGES, EXPERTS, 32, UNIT), BF16),
            pltpu.SemaphoreType.DMA((12,)),
            pltpu.SemaphoreType.DMA((LINKS,)),
            pltpu.SemaphoreType.DMA((LINKS,)),
            pltpu.SemaphoreType.DMA((8,)),
            pltpu.SemaphoreType.DMA((8,)),
        ],
        compiler_params=pltpu.CompilerParams(
            collective_id=0, has_side_effects=True, vmem_limit_bytes=65000 << 10
        ),
        name="layer",
    )(*arrays)


def per_device(
    query_rows,
    key_rows,
    value_rows,
    log_decay,
    attn_gain,
    out_weight,
    residual,
    ffn_gain,
    router,
    expert_ids,
    w_gate,
    w_up,
    w_down,
):
    return layer(
        query_rows,
        key_rows,
        value_rows,
        log_decay.T,
        attn_gain.reshape(1, -1),
        out_weight,
        residual,
        expert_ids.T,
        ffn_gain.reshape(1, -1),
        router.T,
        w_gate[0].T,
        w_up[0].T,
        w_down[0],
    )


def solution(mesh):
    return jax.shard_map(
        per_device,
        mesh=mesh,
        in_specs=(
            P("ctx", "exp"),
            P("ctx", "exp"),
            P("ctx", "exp"),
            P("ctx", "exp"),
            P("exp"),
            P("exp", "ctx"),
            P(("ctx", "exp"), None),
            P(),
            P(),
            P("ctx", None),
            P("exp", None, "ctx"),
            P("exp", None, "ctx"),
            P("exp", "ctx", None),
        ),
        out_specs=P(("ctx", "exp"), None),
        check_vma=False,
    )
```

```python
import functools

import jax
import jax.numpy as jnp
from jax import lax
from jax.experimental import pallas as pl
from jax.experimental.pallas import tpu as pltpu
from jax.sharding import PartitionSpec as P

MESH = pl.DeviceIdType.MESH
F32 = jnp.float32
BF16 = jnp.bfloat16
EXPERTS = 16
CAP = 80
UNIT = 128
STAGES = 3
LINKS = 304


def place():
    ctx = lax.axis_index("ctx")
    exp = lax.axis_index("exp")
    return ctx // 2, ctx % 2, exp // 4, exp % 4


def along(axis, step):
    y, core, x, z = place()
    step = step % 4
    if axis == "x":
        return (y * 2 + core, (x + step) % 4 * 4 + z)
    if axis == "z":
        return (y * 2 + core, x * 4 + (z + step) % 4)
    return ((y + step) % 4 * 2 + core, x * 4 + z)


def exp_peer(step):
    return (lax.axis_index("ctx"), (lax.axis_index("exp") + step) % EXPERTS)


def ctx_peer(step):
    return ((lax.axis_index("ctx") + step) % 8, lax.axis_index("exp"))


def other_core():
    y, core, _, _ = place()
    return (y * 2 + 1 - core, lax.axis_index("exp"))


class Links:
    def __init__(self, send, recv):
        self.send, self.recv, self.count = send, recv, 0
        self.open, self.group, self.early = {}, "w", None

    def copy(self, src, dst, device):
        made = pltpu.make_async_remote_copy(
            src_ref=src,
            dst_ref=dst,
            send_sem=self.send.at[self.count],
            recv_sem=self.recv.at[self.count],
            device_id=device,
            device_id_type=MESH,
        )
        made.start()
        self.count += 1
        assert self.count <= LINKS
        self.open.setdefault(self.group, []).append(made)
        return made

    def drain(self, group):
        for made in self.open.pop(group, []):
            if made is not self.early:
                made.wait_send()


def add_into(target, extra):
    size = 128 if target.shape[0] % 128 == 0 else 80

    def one(i, carry):
        rows = rows_at(i * size, size)
        target[rows, :] = (target[rows, :].astype(F32) + extra[rows, :].astype(F32)).astype(BF16)
        return carry

    lax.fori_loop(0, target.shape[0] // size, one, 0)


class RingSum:
    def __init__(self, links, axis, part, base, n, stride, first, second):
        place_of = dict(zip(("y", "core", "x", "z"), place()))
        self.links, self.axis, self.i = links, axis, place_of[axis]
        self.part, self.base, self.n, self.stride = part, base, n, stride
        self.first, self.second = first, second

    def low(self, d):
        return self.part.at[rows_at(self.base + d * self.stride, self.n // 2)]

    def high(self, d):
        return self.part.at[rows_at(self.base + d * self.stride + self.n // 2, self.n // 2)]

    def slot(self, k):
        return pl.ds(k * (self.n // 2), self.n // 2)

    def opposite(self):
        far, slot = (self.i + 2) % 4, self.slot
        up = self.links.copy(self.low(far), self.first.at[slot(0)], along(self.axis, 1))
        down = self.links.copy(self.high(far), self.first.at[slot(1)], along(self.axis, -1))
        self.far = (up, down)

    def direct_up(self):
        up, slot = (self.i + 1) % 4, self.slot
        self.near = [self.links.copy(self.high(up), self.second.at[slot(1)], along(self.axis, 1))]

    def direct_down(self):
        down, slot = (self.i + 3) % 4, self.slot
        self.near.append(
            self.links.copy(self.low(down), self.second.at[slot(2)], along(self.axis, -1))
        )

    def relay(self):
        up, down, slot = (self.i + 1) % 4, (self.i + 3) % 4, self.slot
        self.far[0].wait_recv()
        add_into(self.low(up), self.first.at[slot(0)])
        self.near.append(
            self.links.copy(self.low(up), self.second.at[slot(0)], along(self.axis, 1))
        )
        self.far[1].wait_recv()
        add_into(self.high(down), self.first.at[slot(1)])
        self.near.append(
            self.links.copy(self.high(down), self.second.at[slot(3)], along(self.axis, -1))
        )

    def arrived(self):
        for made in self.near:
            made.wait_recv()

    def total(self, start, size):
        own = self.part[rows_at(self.base + self.i * self.stride + start, size), :].astype(F32)
        own = own + self.second[rows_at(start, size), :].astype(F32)
        return own + self.second[rows_at(self.n + start, size), :].astype(F32)


class DirectSum:
    def __init__(self, links, axis, part, base, n, landed):
        place_of = dict(zip(("y", "core", "x", "z"), place()))
        self.links, self.axis, self.i = links, axis, place_of[axis]
        self.part, self.base, self.n, self.landed = part, base, n, landed

    def send(self):
        self.moves = [
            self.links.copy(
                self.part.at[rows_at(self.base + (self.i + step) % 4 * self.n, self.n)],
                self.landed.at[pl.ds((step - 1) * self.n, self.n)],
                along(self.axis, step),
            )
            for step in (2, 1, 3)
        ]

    def total(self):
        for made in self.moves:
            made.wait_recv()
        total = self.part[rows_at(self.base + self.i * self.n, self.n), :].astype(F32)
        for k in range(3):
            total = total + self.landed[pl.ds(k * self.n, self.n), :].astype(F32)
        return total


def columns(start, size):
    return pl.ds(pl.multiple_of(start, 128), size)


def rows_at(start, size):
    return pl.ds(pl.multiple_of(start, 16), size)


def split3(value):
    one = value.astype(BF16)
    rest = value - one.astype(F32)
    two = rest.astype(BF16)
    return one, two, (rest - two.astype(F32)).astype(BF16)


def layer_kernel(
    query_ref,
    key_ref,
    value_ref,
    decay_ref,
    head_gain_ref,
    out_w_ref,
    resid_ref,
    ids_ref,
    gain_ref,
    router_ref,
    gate_ref,
    up_ref,
    down_ref,
    out_ref,
    query,
    key,
    value,
    resid,
    routes,
    state,
    chip_state,
    states,
    carried,
    gone,
    attn_ref,
    wide,
    gate_up,
    work,
    second,
    half,
    last,
    resid_parts,
    resid_cols,
    hidden,
    table,
    pieces,
    rows_in,
    tokens,
    scales,
    sums,
    active,
    partner,
    first_y,
    second_y,
    back,
    rows_out,
    local,
    send,
    recv,
    state_send,
    state_recv,
):
    y, core, x, z = place()
    ctx = y * 2 + core
    me = lax.axis_index("exp")
    links = Links(send, recv)
    above, below, far = (y + 1) % 4, (y + 3) % 4, (y + 2) % 4

    def chip_at(home, k):
        return (home + (0, 1, 3, 2)[k]) % 4

    def unit_cols(j):
        k = j // 12
        chip = (y + k + k // 2 - 2 * (k // 3)) % 4
        return columns(chip * 1536 + j % 12 * UNIT, UNIT)

    barrier = pltpu.get_barrier_semaphore()
    for device in [along("y", 1), along("y", 3), other_core(), along("y", 2)]:
        pl.semaphore_signal(barrier, inc=1, device_id=device, device_id_type=MESH)
    for step in range(1, EXPERTS):
        pl.semaphore_signal(barrier, inc=1, device_id=exp_peer(step), device_id_type=MESH)

    load_gate = pltpu.make_async_copy(gate_ref, gate_up.at[pl.ds(0, 576)], local.at[1])
    load_up = pltpu.make_async_copy(up_ref, gate_up.at[pl.ds(576, 576)], local.at[2])
    w_all, w_low, w_high = pl.ds(0, 512), pl.ds(0, 256), pl.ds(256, 256)
    one_way, other_way = (2 * core + 3) % 4, (2 * core + 1) % 4
    one_chip, other_chip = (y + one_way) % 4, (y + other_way) % 4

    def w_part(chip, side, rows):
        return wide.at[chip, rows, columns(side * 768, 768)]

    load_in = []
    for k, (src, dst) in enumerate(
        (
            (key_ref, key),
            (value_ref, value),
            (query_ref, query),
            (resid_ref, resid),
            (router_ref, routes),
        )
    ):
        made = pltpu.make_async_copy(src, dst, local.at[7 + k])
        made.start()
        load_in.append(made)
    load_w = pltpu.make_async_copy(out_w_ref, w_part(y, core, w_all), local.at[0])
    load_w.start()

    earlier = lax.broadcasted_iota(jnp.int32, (512, 512), 1) <= lax.broadcasted_iota(
        jnp.int32, (512, 512), 0
    )
    lower = jnp.where(earlier, 1.0, 0.0).astype(BF16)
    turned = (((1,), (1,)), ((), ()))
    first = (((0,), (0,)), ((), ()))
    run_col = jnp.zeros((512, 4), F32)
    run_row = jnp.zeros((4, 512), F32)
    for term in split3(decay_ref[...]):
        run_col = run_col + lax.dot_general(lower, term, turned, preferred_element_type=F32)
        run_row = run_row + lax.dot_general(term, lower, turned, preferred_element_type=F32)
    load_in[0].wait()
    load_in[1].wait()
    lines = lax.broadcasted_iota(jnp.int32, (4, 128), 0)
    ends = jnp.zeros((4, 128), F32)
    for h in range(4):
        lanes = pl.ds(h * 128, 128)
        end = run_col[511:512, h : h + 1]
        to_end = jnp.exp(end - run_col[:, h : h + 1])
        decayed = (key[:, lanes].astype(F32) * to_end).astype(BF16)
        own = lax.dot_general(decayed, value[:, lanes], first, preferred_element_type=F32)
        state[pl.ds(h * 128, 128), :] = own.astype(BF16)
        ends = jnp.where(lines == h, end, ends)

    def pack_ends(value):
        parts = [t.astype(F32) for t in split3(value)]
        return jnp.concatenate(parts + [jnp.zeros((4, 128), F32)], axis=0).astype(BF16)

    def ends_of(ref):
        value = ref[pl.ds(512, 16), :].astype(F32)
        return value[0:4] + value[4:8] + value[8:12]

    state[pl.ds(512, 16), :] = pack_ends(ends)

    pl.semaphore_wait(barrier, EXPERTS + 3)

    def state_copy(src, dst, k, device):
        return pltpu.make_async_remote_copy(
            src_ref=src,
            dst_ref=dst,
            send_sem=state_send.at[k],
            recv_sem=state_recv.at[k],
            device_id=device,
            device_id_type=MESH,
        )

    def state_pair():
        return state_copy(state, states.at[0], 0, other_core())

    def state_up(step):
        return state_copy(chip_state, states.at[step], step, along("y", step))

    def state_over(step):
        return state_copy(states.at[step], states.at[step], 4 + step, other_core())

    state_pair().start()

    def spread_w(chip, rows, device):
        src = out_w_ref if chip is None else w_part(chip, core, rows)
        return links.copy(src, w_part(y if chip is None else chip, core, rows), device)

    w_first = spread_w(None, w_all, along("y", one_way))
    w_pair = [spread_w(None, w_all, other_core())]

    state_pair().wait_recv()

    @pl.when(core == 0)
    def _():
        pair_ends = ends_of(states.at[0])
        for h in range(4):
            rows = pl.ds(h * 128, 128)
            joined = jnp.exp(pair_ends[h : h + 1]) * state[rows, :].astype(F32)
            chip_state[rows, :] = (joined + states[0, rows, :].astype(F32)).astype(BF16)
        chip_state[pl.ds(512, 16), :] = pack_ends(pair_ends + ends_of(state))
        for step in range(1, 4):

            @pl.when(y + step < 4)
            def _(step=step):
                state_up(step).start()

    load_gate.start()
    load_up.start()

    for made in load_in[2:]:
        made.wait()

    def resid_part(g, carry):
        for s in range(STAGES):
            resid_parts[g, :, pl.ds(s * UNIT, UNIT)] = resid[:, unit_cols(s * EXPERTS + g)]
        return carry

    lax.fori_loop(0, EXPERTS, resid_part, 0)
    resid_moves = []
    links.group = "rows"
    for step in range(1, EXPERTS):
        to = (me + step) % EXPERTS
        resid_moves.append(
            links.copy(resid_parts.at[to], resid_cols.at[rows_at(me * 32, 32)], exp_peer(step))
        )
    resid_cols[rows_at(me * 32, 32), :] = resid_parts[me]

    for h in range(4):
        lanes = pl.ds(h * 128, 128)
        for r in range(2):
            seen = (r + 1) * 256
            rows = pl.ds(r * 256, 256)
            scores = lax.dot_general(
                query[rows, lanes],
                key[pl.ds(0, seen), lanes],
                turned,
                preferred_element_type=F32,
            )
            spread_of = run_col[r * 256 : seen, h : h + 1] - run_row[h : h + 1, :seen]
            late = lax.broadcasted_iota(jnp.int32, (256, seen), 0) + r * 256
            soon = lax.broadcasted_iota(jnp.int32, (256, seen), 1)
            decay = jnp.where(late >= soon, jnp.exp(jnp.minimum(spread_of, 0.0)), 0.0)
            sums[rows, lanes] = jnp.dot(
                (scores * decay).astype(BF16),
                value[pl.ds(0, seen), lanes],
                preferred_element_type=F32,
            )

    for step in range(1, 4):

        @pl.when((core == 0) & (y >= step))
        def _(step=step):
            state_up(step).wait_recv()
            state_over(step).start()

    links.group = "w"
    w_first.wait_send()
    links.early = w_first
    w_second = spread_w(None, w_all, along("y", other_way))
    w_first.wait_recv()
    w_near = spread_w(other_chip, w_all, other_core())
    w_far = [spread_w(other_chip, w_low, along("y", one_way))]

    experts = lax.broadcasted_iota(jnp.int32, (EXPERTS, 512), 0)
    picked = (ids_ref[0:1, :] == experts) | (ids_ref[1:2, :] == experts)
    before = lax.broadcasted_iota(jnp.int32, (512, 512), 0) < lax.broadcasted_iota(
        jnp.int32, (512, 512), 1
    )
    rank = jnp.dot(
        jnp.where(picked, 1.0, 0.0).astype(BF16),
        jnp.where(before, 1.0, 0.0).astype(BF16),
        preferred_element_type=F32,
    )
    code = jnp.where(picked, rank, -1.0)
    slots = lax.broadcasted_iota(jnp.int32, (CAP, 512), 0).astype(F32)
    for e in range(EXPERTS):
        table[pl.ds(e * CAP, CAP), :] = jnp.where(code[e : e + 1, :] == slots, 1.0, 0.0).astype(
            BF16
        )

    carried[...] = jnp.zeros((512, 128), F32)
    gone[...] = jnp.zeros((4, 128), F32)
    for step in range(1, 4):

        @pl.when((core == 1) & (y >= step))
        def _(step=step):
            state_over(step).wait_recv()

        @pl.when(y >= step)
        def _(step=step):
            for h in range(4):
                rows = pl.ds(h * 128, 128)
                kept = jnp.exp(gone[pl.ds(h, 1), :])
                carried[rows, :] = carried[rows, :] + kept * states[step, rows, :].astype(F32)
            gone[...] = gone[...] + ends_of(states.at[step])

    @pl.when(core == 1)
    def _():
        pair_ends = ends_of(states.at[0])
        for h in range(4):
            rows = pl.ds(h * 128, 128)
            kept = jnp.exp(pair_ends[h : h + 1])
            carried[rows, :] = kept * carried[rows, :] + states[0, rows, :].astype(F32)

    for h in range(4):
        lanes = pl.ds(h * 128, 128)
        full = carried[lanes, :]
        near = full.astype(BF16)
        rest = (full - near.astype(F32)).astype(BF16)
        asked = query[:, lanes]
        cross = jnp.dot(asked, near, preferred_element_type=F32)
        cross = cross + jnp.dot(asked, rest, preferred_element_type=F32)
        total = sums[pl.ds(0, 512), lanes] + jnp.exp(run_col[:, h : h + 1]) * cross
        mean = jnp.mean(total * total, axis=1, keepdims=True)
        attn_ref[:, lanes] = (
            total * lax.rsqrt(mean + 1e-06) * head_gain_ref[:, lanes]
        ).astype(BF16)

    load_w.wait()
    w_near.wait_recv()
    for made in w_pair:
        made.wait_recv()

    rings_a, rings_b, lasts_a, lasts_b = [], [], [], []
    for s in range(STAGES):
        for which, (rings, axis) in enumerate(((rings_a, "x"), (rings_b, "z"))):
            k = which * STAGES + s
            rings.append(
                RingSum(
                    links,
                    axis,
                    work,
                    k * 4096,
                    1024,
                    1024,
                    work.at[pl.ds(6 * 4096 + k * 1024, 1024)],
                    second.at[pl.ds(k * 2048, 2048)],
                )
            )
        for which, (sums_of, axis) in enumerate(((lasts_a, "z"), (lasts_b, "x"))):
            k = which * STAGES + s
            sums_of.append(
                DirectSum(links, axis, half, k * 1024, 256, last.at[pl.ds(k * 768, 768)])
            )

    def project_quad(s, to):
        quad = s * 4 + to
        k = quad // 3
        chip = (y + k + k // 2 - 2 * (k // 3)) % 4
        w = wide[chip, pl.ds(0, 512), columns(quad % 3 * 512, 512)]
        r = jnp.dot(attn_ref[...], w, preferred_element_type=F32).astype(BF16)
        for u in range(4):
            for side in range(2):
                start = s * 4096 + to * 1024 + (side * 4 + u) * 128
                work[rows_at(start, 128), :] = r[
                    side * 128 : side * 128 + 128, u * UNIT : u * UNIT + UNIT
                ]
                start = (STAGES + s) * 4096 + u * 1024 + (side * 4 + to) * 128
                work[rows_at(start, 128), :] = r[
                    256 + side * 128 : 256 + side * 128 + 128, u * UNIT : u * UNIT + UNIT
                ]

    def project(s):
        def one(i, carry):
            project_quad(s, (x + 3 + i) % 4)
            return carry

        links.group = "sum"
        project_quad(s, (x + 2) % 4)
        rings_a[s].opposite()
        lax.fori_loop(0, 3, one, 0)
        rings_b[s].opposite()
        rings_a[s].direct_up()
        rings_a[s].direct_down()
        rings_b[s].direct_up()
        rings_b[s].direct_down()

    def relay(s):
        links.group = "sum"
        rings_a[s].relay()
        rings_b[s].relay()

    def turn(s):
        links.group = "sum"
        for ring, last_of in ((rings_a[s], lasts_a[s]), (rings_b[s], lasts_b[s])):
            ring.arrived()

            def one(u, carry, ring=ring, last_of=last_of):
                for side in range(2):
                    rows = rows_at(last_of.base + u * 256 + side * 128, 128)
                    half[rows, :] = ring.total(side * 512 + u * 128, 128).astype(BF16)
                return carry

            lax.fori_loop(0, 4, one, 0)
            last_of.send()

    row_moves = [[] for _ in range(STAGES)]
    block = EXPERTS * CAP

    def dispatch(s):
        cols = pl.ds(s * UNIT, UNIT)
        if s == 0:
            for made in resid_moves:
                made.wait_recv()
        links.group = "rows"
        for start, last_of in ((0, lasts_a[s]), (256, lasts_b[s])):
            total = last_of.total() + resid_cols[pl.ds(start, 256), cols].astype(F32)
            hidden[pl.ds(s * 512 + start, 256), :] = total.astype(BF16)
        found = jnp.dot(table[...], hidden[pl.ds(s * 512, 512), :], preferred_element_type=F32)
        pieces[pl.ds(s * block, block), :] = found.astype(BF16)
        lands = rows_in.at[rows_at((s * EXPERTS + me) * CAP, CAP)]
        for step in range(1, EXPERTS):
            to = (me + step) % EXPERTS
            piece = pieces.at[rows_at((s * EXPERTS + to) * CAP, CAP)]
            row_moves[s].append(links.copy(piece, lands, exp_peer(step)))
        lands[...] = pieces[rows_at((s * EXPERTS + me) * CAP, CAP), :]

    squares = [jnp.zeros((CAP, 1), F32)]
    mine = rows_at(ctx * CAP, CAP)
    gathers = [None] * STAGES

    def spread(s, block, side, device):
        cols = pl.ds(s * 2048 + side * 1024, 1024)
        if side == 2:
            cols = pl.ds(s * 2048, 2048)
        ref = tokens.at[rows_at(block * CAP, CAP), cols]
        return links.copy(ref, ref, device)

    def gather(s):
        for made in row_moves[s]:
            made.wait_recv()
        links.group = "gather"
        for u in range(EXPERTS):
            cols = pl.ds((s * EXPERTS + u) * UNIT, UNIT)
            part = rows_in[pl.ds((s * EXPERTS + u) * CAP, CAP), :].astype(F32)
            squares[0] = squares[0] + jnp.sum(part * part, axis=1, keepdims=True)
            tokens[mine, cols] = (part * gain_ref[:, unit_cols(s * EXPERTS + u)]).astype(BF16)
        gathers[s] = dict(
            up_low=spread(s, ctx, 0, along("y", 1)),
            down_high=spread(s, ctx, 1, along("y", -1)),
            pair=[spread(s, ctx, 2, other_core())],
        )

    def gather_late(s):
        links.group = "gather"
        gathers[s]["up_high"] = spread(s, ctx, 1, along("y", 1))
        gathers[s]["down_low"] = spread(s, ctx, 0, along("y", -1))

    from_below, from_above, from_far = below * 2 + core, above * 2 + core, far * 2 + core

    def gather_mid(s):
        links.group = "gather"
        g = gathers[s]
        g["up_low"].wait_recv()
        g["on_up"] = spread(s, from_below, 0, along("y", 1))
        g["near"] = [spread(s, from_below, 0, other_core())]
        g["down_high"].wait_recv()
        g["on_down"] = spread(s, from_above, 1, along("y", -1))
        g["near"].append(spread(s, from_above, 1, other_core()))

    def gather_near(s):
        links.group = "gather"
        g = gathers[s]
        g["up_high"].wait_recv()
        g["near"].append(spread(s, from_below, 1, other_core()))
        g["down_low"].wait_recv()
        g["near"].append(spread(s, from_above, 0, other_core()))

    def gather_far(s):
        links.group = "gather"
        g = gathers[s]
        g["on_up"].wait_recv()
        g["far"] = [spread(s, from_far, 0, other_core())]
        g["on_down"].wait_recv()
        g["far"].append(spread(s, from_far, 1, other_core()))

    def held(s, names):
        for name in names:
            for made in gathers[s][name]:
                made.wait_recv()

    def gate_and_up(s, chip):
        rows = rows_at(chip * (2 * CAP), 2 * CAP)
        total = None
        quad = s * 4
        while quad < s * 4 + 4:
            run = min(3 - quad % 3, s * 4 + 4 - quad)
            start = columns(chip_at(chip, quad // 3) * 1536 + quad % 3 * 512, run * 512)
            part = lax.dot_general(
                tokens[rows, pl.ds(quad * 512, run * 512)],
                gate_up[:, start],
                turned,
                preferred_element_type=F32,
            )
            total = part if total is None else total + part
            quad += run
        if s > 0:
            total = total + sums[rows, :]
        if s < STAGES - 1:
            sums[rows, :] = total
            return
        total = total * scales[rows, 0:1]
        gate, upper = total[:, :576], total[:, 576:]
        active[...] = (gate / (1.0 + jnp.exp(-gate)) * upper).astype(BF16)

    project(0)
    relay(0)
    links.group = "w"
    w_second.wait_recv()
    w_next = spread_w(one_chip, w_all, other_core())
    w_far.append(spread_w(one_chip, w_high, along("y", other_way)))
    w_next.wait_recv()
    project(1)
    turn(0)
    links.group = "w"
    w_far_near = []
    for made, rows in zip(w_far, (w_low, w_high)):
        made.wait_recv()
        w_far_near.append(spread_w(far, rows, other_core()))
    relay(1)
    dispatch(0)
    turn(1)
    for made in w_far_near:
        made.wait_recv()
    project(2)
    gather(0)
    dispatch(1)
    gather_late(0)
    relay(2)
    gather_mid(0)
    gather(1)
    turn(2)
    gather_late(1)
    gather_near(0)
    gather_far(0)
    gather_mid(1)
    dispatch(2)
    links.drain("w")
    load_down = []
    for k in range(4):
        made = pltpu.make_async_copy(
            down_ref.at[:, pl.ds(k * 1536, 1536)], wide.at[k], local.at[3 + k]
        )
        made.start()
        load_down.append(made)
    load_gate.wait()
    load_up.wait()
    held(0, ("pair", "near", "far"))
    gate_and_up(0, y)
    gate_and_up(0, above)
    gather_near(1)
    gate_and_up(0, below)
    gather_far(1)
    gather(2)

    def spread_scale(block, device):
        ref = scales.at[rows_at(block * CAP, CAP)]
        return links.copy(ref, ref, device)

    scale = lax.rsqrt(squares[0] / 6144.0 + 1e-05)
    scales[mine, :] = jnp.broadcast_to(scale, (CAP, UNIT))
    scale_up = spread_scale(ctx, along("y", 1))
    scale_down = spread_scale(ctx, along("y", -1))
    scale_own = spread_scale(ctx, other_core())
    def owned(owner, chip, s):
        return work.at[rows_at(((owner * 4 + chip) * STAGES + s) * block, block)]

    def down(chip, between=None):
        moves = []
        for s in range(STAGES):

            def one(quad, carry):
                k = quad // 3
                part = (chip + k + k // 2 - 2 * (k // 3)) % 4
                w = wide[part, :, columns(quad % 3 * 512, 512)]
                o = jnp.dot(active[...], w, preferred_element_type=F32).astype(BF16)
                for owner in range(2):
                    for u in range(4):
                        start = (owner * 4 + chip) * (STAGES * block) + (quad * 4 + u) * CAP
                        work[rows_at(start, CAP), :] = o[
                            owner * CAP : owner * CAP + CAP, u * UNIT : u * UNIT + UNIT
                        ]
                return carry

            lax.fori_loop(4 * s, 4 * s + 4, one, 0)
            lands = partner.at[rows_at((chip * STAGES + s) * block, block)]
            moves.append(links.copy(owned(1 - core, chip, s), lands, other_core()))
            if between is not None and s > 0:
                join(chip, moves, s - 1)
                between(s - 1)
        return moves

    def join(chip, moves, s):
        moves[s].wait_recv()
        add_into(owned(core, chip, s), partner.at[rows_at((chip * STAGES + s) * block, block)])

    rings_y = [
        RingSum(
            links,
            "y",
            work,
            core * (4 * STAGES * block) + s * block,
            block,
            STAGES * block,
            first_y.at[pl.ds(s * block, block)],
            second_y.at[pl.ds(s * 2 * block, 2 * block)],
        )
        for s in range(STAGES)
    ]
    held(1, ("pair", "near", "far"))
    gate_and_up(1, y)
    held(2, ("pair",))
    scale_own.wait_recv()
    gate_and_up(2, y)
    gather_late(2)
    gather_mid(2)
    scale_up.wait_recv()
    scale_on = spread_scale(from_below, along("y", 1))
    scale_pair = [spread_scale(from_below, other_core())]
    scale_down.wait_recv()
    scale_pair.append(spread_scale(from_above, other_core()))
    links.drain("sum")
    for made in load_down:
        made.wait()
    links.group = "rest"
    sum_own = down(y)
    gather_near(2)
    scale_on.wait_recv()
    scale_far = spread_scale(from_far, other_core())
    gate_and_up(0, far)
    gate_and_up(1, far)
    gather_far(2)
    links.group = "rest"
    gate_and_up(1, above)
    held(2, ("far",))
    scale_far.wait_recv()
    gate_and_up(2, far)
    def far_ready(s):
        rings_y[s].opposite()

    def above_ready(s):
        rings_y[s].direct_up()

    def below_ready(s):
        rings_y[s].direct_down()
        if s == 0:
            rings_y[0].relay()

    sum_far = down(far, far_ready)
    held(2, ("near",))
    for made in scale_pair:
        made.wait_recv()
    gate_and_up(2, above)
    join(far, sum_far, 2)
    rings_y[2].opposite()
    sum_above = down(above, above_ready)
    gate_and_up(1, below)
    gate_and_up(2, below)
    join(above, sum_above, 2)
    sum_below = down(below, below_ready)
    join(below, sum_below, 2)
    for s in range(STAGES):
        join(y, sum_own, s)

    my_ids = lax.dot_general(
        table[rows_at(me * CAP, CAP), :],
        ids_ref[...].astype(F32).astype(BF16),
        turned,
        preferred_element_type=F32,
    )
    logits = jnp.zeros((CAP, EXPERTS), F32)
    for k in range(4):
        part = routes[:, columns(chip_at(y, k) * 1536, 1536)]
        router_high = part.astype(BF16)
        router_low = (part - router_high.astype(F32)).astype(BF16)
        token = tokens[mine, pl.ds(k * 1536, 1536)]
        for w in (router_high, router_low):
            logits = logits + lax.dot_general(token, w, turned, preferred_element_type=F32)
    gates = 1.0 / (1.0 + jnp.exp(-logits * scale))
    lanes = lax.broadcasted_iota(jnp.int32, (CAP, EXPERTS), 1)
    lanes_f = lanes.astype(F32)
    both = (my_ids[:, 0:1] == lanes_f) | (my_ids[:, 1:2] == lanes_f)
    total = jnp.sum(jnp.where(both, gates, 0.0), axis=1, keepdims=True)
    share = jnp.sum(jnp.where(lanes == me, gates, 0.0), axis=1, keepdims=True) / total
    share = jnp.broadcast_to(share, (CAP, UNIT))

    links.drain("rows")

    back_moves = [[] for _ in range(STAGES)]
    out_moves = []

    def give_back(s):
        rings_y[s].arrived()

        lands = back.at[rows_at((s * EXPERTS + me) * CAP, CAP)]
        for step in list(range(1, EXPERTS)) + [0]:
            to = (me + step) % EXPERTS
            total = rings_y[s].total(to * CAP, CAP).astype(BF16).astype(F32)
            piece = pieces.at[rows_at((s * EXPERTS + to) * CAP, CAP)]
            if step == 0:
                lands[...] = (total * share).astype(BF16)
                continue
            piece[...] = (total * share).astype(BF16)
            back_moves[s].append(links.copy(piece, lands, exp_peer(step)))

    def combine(s):
        for made in back_moves[s]:
            made.wait_recv()
        summed = lax.dot_general(
            table[...], back[pl.ds(s * block, block), :], first, preferred_element_type=F32
        )
        rows = pl.ds(s * 512, 512)
        hidden[rows, :] = (hidden[rows, :].astype(F32) + summed).astype(BF16)
        for step in range(1, EXPERTS):
            to = (me + step) % EXPERTS
            part = hidden.at[rows_at(s * 512 + to * 32, 32)]
            out_moves.append(links.copy(part, rows_out.at[s, me], exp_peer(step)))
        rows_out[s, me] = hidden[rows_at(s * 512 + me * 32, 32), :]

    rings_y[1].relay()
    rings_y[2].direct_up()
    rings_y[2].direct_down()
    give_back(0)
    rings_y[2].relay()
    give_back(1)
    combine(0)
    give_back(2)
    combine(1)
    combine(2)
    for made in out_moves:
        made.wait_recv()

    def put(g, carry):
        for s in range(STAGES):
            out_ref[:, unit_cols(s * EXPERTS + g)] = rows_out[s, g]
        return carry

    lax.fori_loop(0, EXPERTS, put, 0)
    links.drain("gather")
    links.drain("rest")

    state_pair().wait_send()

    for step in range(1, 4):

        @pl.when((core == 0) & (y + step < 4))
        def _(step=step):
            state_up(step).wait_send()

        @pl.when((core == 0) & (y >= step))
        def _(step=step):
            state_over(step).wait_send()


def layer(*arrays):
    vmem = pl.BlockSpec(memory_space=pltpu.VMEM)
    hbm = pl.BlockSpec(memory_space=pl.ANY)

    def rows(n, width=UNIT):
        return pltpu.VMEM((n, width), BF16)

    block = EXPERTS * CAP
    return pl.pallas_call(
        layer_kernel,
        out_shape=jax.ShapeDtypeStruct((32, 6144), BF16),
        in_specs=[hbm] * 3 + [vmem] * 2 + [hbm] * 2 + [vmem] * 2 + [hbm] * 4,
        out_specs=vmem,
        scratch_shapes=[
            rows(512, 512),
            rows(512, 512),
            rows(512, 512),
            rows(32, 6144),
            pltpu.VMEM((EXPERTS, 6144), F32),
            rows(528),
            rows(528),
            pltpu.VMEM((4, 528, 128), BF16),
            pltpu.VMEM((512, 128), F32),
            pltpu.VMEM((4, 128), F32),
            rows(512, 512),
            pltpu.VMEM((4, 576, 1536), BF16),
            rows(1152, 6144),
            rows(24 * block),
            rows(6 * 2048),
            rows(6 * 1024),
            rows(6 * 768),
            pltpu.VMEM((EXPERTS, 32, STAGES * UNIT), BF16),
            rows(512, STAGES * UNIT),
            rows(STAGES * 512),
            rows(block, 512),
            rows(STAGES * block),
            rows(STAGES * block),
            rows(8 * CAP, 6144),
            pltpu.VMEM((8 * CAP, UNIT), F32),
            pltpu.VMEM((8 * CAP, 1152), F32),
            rows(2 * CAP, 576),
            rows(4 * STAGES * block),
            rows(STAGES * block),
            rows(2 * STAGES * block),
            rows(STAGES * block),
            pltpu.VMEM((STAGES, EXPERTS, 32, UNIT), BF16),
            pltpu.SemaphoreType.DMA((12,)),
            pltpu.SemaphoreType.DMA((LINKS,)),
            pltpu.SemaphoreType.DMA((LINKS,)),
            pltpu.SemaphoreType.DMA((8,)),
            pltpu.SemaphoreType.DMA((8,)),
        ],
        compiler_params=pltpu.CompilerParams(
            collective_id=0, has_side_effects=True, vmem_limit_bytes=65000 << 10
        ),
        name="layer",
    )(*arrays)


def per_device(
    query_rows,
    key_rows,
    value_rows,
    log_decay,
    attn_gain,
    out_weight,
    residual,
    ffn_gain,
    router,
    expert_ids,
    w_gate,
    w_up,
    w_down,
):
    return layer(
        query_rows,
        key_rows,
        value_rows,
        log_decay.T,
        attn_gain.reshape(1, -1),
        out_weight,
        residual,
        expert_ids.T,
        ffn_gain.reshape(1, -1),
        router.T,
        w_gate[0].T,
        w_up[0].T,
        w_down[0],
    )


def solution(mesh):
    return jax.shard_map(
        per_device,
        mesh=mesh,
        in_specs=(
            P("ctx", "exp"),
            P("ctx", "exp"),
            P("ctx", "exp"),
            P("ctx", "exp"),
            P("exp"),
            P("exp", "ctx"),
            P(("ctx", "exp"), None),
            P(),
            P(),
            P("ctx", None),
            P("exp", None, "ctx"),
            P("exp", None, "ctx"),
            P("exp", "ctx", None),
        ),
        out_specs=P(("ctx", "exp"), None),
        check_vma=False,
    )
```
